512 devices in a mesh: row: 64 (over y, z), col: 8 (over x, core).
Axes of the slice: x: 4, y: 4, z: 16, core: 2. Of those that a mesh axis runs over, the one named last changes fastest.
Arguments:
- earlier_vectors: bfloat16 [16384, 1536], P(('row', 'col')), may hold values from -0.4082483 to 0.4082483
- later_vectors: bfloat16 [8192, 1536], P(('row', 'col')), may hold values from -0.4082483 to 0.4082483
Outputs:
- mixed_dual_left: float32 [16384], P(('row', 'col'))
- mixed_dual_right: float32 [8192], P(('row', 'col'))
- earlier_symmetric_dual: float32 [16384], P(('row', 'col'))
- later_symmetric_dual: float32 [8192], P(('row', 'col'))
- divergence: float32 [], replicated
The draws below stay inside these ranges and needn't reach their ends.
All inputs are finite; a program needn't handle non-finite values.
Results may differ from the reference program's by a relative error of at most 0.0003.
Values may be sent and summed in bfloat16 or wider, within the bound.
A program may use at most 64 MiB of HBM per device.

```python
import math
import jax
import jax.numpy as jnp
from jax import lax

D = 1536
ITERS = 2
N = 16384
M = 8192


def shared_layout(key):
    layout_key = jax.random.fold_in(key, 202)
    centre_key, radius_key, width_key = jax.random.split(layout_key, 3)
    groups = max(N // 256, 2)
    spread = jax.random.uniform(width_key, (1, D), jnp.float32, 0.0, math.log(16.0))
    widths = jnp.exp(0.5 * spread) / math.sqrt(15.0 / math.log(16.0))
    radii = jnp.sqrt(jnp.exp(jax.random.uniform(radius_key, (groups, 1), jnp.float32, math.log(0.15), math.log(1.2))))
    centres = jax.random.truncated_normal(centre_key, -3.0, 3.0, (groups, D), jnp.float32) * widths * radii / D ** 0.5
    return (centres, widths)


def place_rows(key, count, centres, widths, base):
    pick_key, radius_key = jax.random.split(key, 2)
    groups = centres.shape[0]
    members = jax.random.randint(pick_key, (count,), 0, groups)
    radii = jnp.sqrt(jnp.exp(jax.random.uniform(radius_key, (count, 1), jnp.float32, math.log(0.03), math.log(0.24))))
    return jnp.take(centres, members, axis=0) + base * widths * radii / D ** 0.5


def distant_rows(key, values):
    far_key = jax.random.fold_in(key, 303)
    signs = jnp.where(jax.random.uniform(far_key, (1, D), jnp.float32) < 0.5, -1.0, 1.0)
    strengths = jnp.array([2.8, 3.6, 4.4, 5.2], jnp.float32)[:, None]
    shifted = values[16:20] + strengths * signs / D ** 0.5
    return values.at[16:20].set(shifted)


def draw_earlier_vectors(key, part):
    centres, widths = shared_layout(key)
    key = jax.random.fold_in(key, 11)
    noise_key, place_key = jax.random.split(key, 2)
    base = jax.random.truncated_normal(noise_key, -3.5, 3.5, (N, D), jnp.float32)
    values = place_rows(place_key, N, centres, widths, base)
    values = distant_rows(key, values)
    return jnp.clip(values, -15.5 / D ** 0.5, 15.5 / D ** 0.5).astype(jnp.bfloat16)


def draw_later_vectors(key, part):
    centres, widths = shared_layout(key)
    key = jax.random.fold_in(key, 23)
    noise_key, place_key, drift_key = jax.random.split(key, 3)
    drift = jax.random.truncated_normal(drift_key, -3.0, 3.0, centres.shape, jnp.float32) * widths * (0.22 / D ** 0.5)
    shifted = centres + drift
    base = jax.random.truncated_normal(noise_key, -3.5, 3.5, (M, D), jnp.float32)
    values = place_rows(place_key, M, shifted, widths, base)
    values = distant_rows(key, values)
    return jnp.clip(values, -15.5 / D ** 0.5, 15.5 / D ** 0.5).astype(jnp.bfloat16)


def setup_inputs(seed: int = 0) -> dict:
    splits = jax.random.split(jax.random.key(seed), 3)
    return {
        "earlier_vectors": draw_earlier_vectors(jax.random.fold_in(splits[2], 71), 0),
        "later_vectors": draw_later_vectors(jax.random.fold_in(splits[2], 71), 0),
    }


EPSILON = 0.04


def cost_block(source_weights, target_weights, row_norms, col_norms):
    cross = jnp.dot(source_weights, target_weights.T, preferred_element_type=jnp.float32)
    return 0.5 * row_norms[:, None] + 0.5 * col_norms[None, :] - cross


def entropic_transport_routine(source_weights, target_weights):
    count_rows = source_weights.shape[0]
    count_cols = target_weights.shape[0]
    block = math.gcd(count_rows, 512)
    row_norms = jnp.sum(jnp.square(source_weights.astype(jnp.float32)), axis=1)
    col_norms = jnp.sum(jnp.square(target_weights.astype(jnp.float32)), axis=1)
    log_rows = -jnp.log(jnp.float32(count_rows))
    log_cols = -jnp.log(jnp.float32(count_cols))
    rows_split = source_weights.reshape(count_rows // block, block, source_weights.shape[1])
    norms_split = row_norms.reshape(count_rows // block, block)

    def one_iter(col_pot):
        def step(carry, item):
            best, total = carry
            part, part_norms = item
            cost = cost_block(part, target_weights, part_norms, col_norms)
            score = (col_pot[None, :] - cost) / EPSILON
            top = jnp.max(score, axis=1)
            row_pot = -EPSILON * (log_cols + top + jnp.log(jnp.sum(jnp.exp(score - top[:, None]), axis=1)))
            back = (row_pot[:, None] - cost) / EPSILON
            new_best = jnp.maximum(best, jnp.max(back, axis=0))
            new_total = total * jnp.exp(best - new_best) + jnp.sum(jnp.exp(back - new_best[None, :]), axis=0)
            return (new_best, new_total), row_pot

        start = (jnp.full((count_cols,), -1e30, jnp.float32), jnp.zeros((count_cols,), jnp.float32))
        (best, total), row_pot = lax.scan(step, start, (rows_split, norms_split))
        new_col = -EPSILON * (log_rows + best + jnp.log(total))
        return row_pot.reshape(count_rows), new_col

    col_pot = jnp.zeros((count_cols,), jnp.float32)
    row_pot = jnp.zeros((count_rows,), jnp.float32)
    for step_index in range(ITERS):
        row_pot, col_pot = one_iter(col_pot)
    value = jnp.mean(row_pot) + jnp.mean(col_pot)
    return row_pot, col_pot, value


def reference(earlier_vectors, later_vectors):
    mixed_dual_left, mixed_dual_right, mixed_transport_objective = entropic_transport_routine(earlier_vectors, later_vectors)
    earlier_symmetric_dual, unused_earlier_dual, earlier_symmetric_objective = entropic_transport_routine(earlier_vectors, earlier_vectors)
    later_symmetric_dual, unused_later_dual, later_symmetric_objective = entropic_transport_routine(later_vectors, later_vectors)
    divergence = mixed_transport_objective - 0.5 * earlier_symmetric_objective - 0.5 * later_symmetric_objective
    return mixed_dual_left, mixed_dual_right, earlier_symmetric_dual, later_symmetric_dual, divergence
```

```python
import functools

import jax
import jax.numpy as jnp
import numpy as np
from jax import lax
from jax.experimental import pallas as pl
from jax.experimental.pallas import tpu as pltpu
from jax.sharding import PartitionSpec as P

EPSILON = 0.04
ITERS = 2
MESH = pl.DeviceIdType.MESH

NX, NY, NZ = 4, 4, 16
PLANE = NX * NY
HALF = NZ // 2
NEAR = 4
FAR = NZ // NEAR
UNIT = 16
UNITS = 3
TILE = 256
STEP = 128
SCALE = float(np.log2(np.e)) / EPSILON


def add(a, b):
    return a + b


def tree(op, parts):
    while len(parts) > 1:
        parts = [op(parts[i], parts[i + 1]) for i in range(0, len(parts) - 1, 2)] + (
            [parts[-1]] if len(parts) % 2 else []
        )
    return parts[0]


def fold_rows(x, op):
    return tree(op, [x[8 * k : 8 * k + 8] for k in range(x.shape[0] // 8)])


def each(lower, upper, body):
    def step(k, carry):
        body(k)
        return carry

    lax.fori_loop(lower, upper, step, 0)


def kernel(
    src_ref,
    tgt_ref,
    out_ref,
    rows,
    cols,
    scores,
    best,
    acc,
    acc_cross,
    pot,
    col_pot,
    phi_ref,
    totals,
    row_send,
    row_recv,
    near_send,
    near_recv,
    far_send,
    far_recv,
    sum_send,
    sum_recv,
    own_sem,
    z_rs,
    sib_rs,
    first_rs,
    second_rs,
    onward_rs,
    gather_ss,
    row_ss,
    row_rs,
    near_ss,
    near_rs,
    far_ss,
    far_rs,
    sum_ss,
    sum_rs,
):
    a, width = src_ref.shape
    b = tgt_ref.shape[0]
    n_src, n_tgt = a * PLANE * NZ * 2, b * PLANE * NZ * 2
    log_src, log_tgt = float(np.log2(n_src)), float(np.log2(n_tgt))
    rows_src, rows_tgt = a * PLANE, b * PLANE
    cols_src, cols_tgt = a * NZ * 2, b * NZ * 2
    last = cols_src + cols_tgt
    lanes_src, lanes_tgt = cols_src // 128, cols_tgt // 128
    blocks_src, blocks_tgt = rows_src // 128, rows_tgt // 128

    row, col = lax.axis_index("row"), lax.axis_index("col")
    y, z = lax.div(row, NZ), lax.rem(row, NZ)
    x, core = lax.div(col, 2), lax.rem(col, 2)
    other = 1 - core
    place = y * NX + x

    def device(xx, yy, zz, cc):
        return (yy * NZ + zz, xx * 2 + cc)

    def remote(src, dst, ss, rs, to):
        return pltpu.make_async_remote_copy(
            src_ref=src, dst_ref=dst, send_sem=ss, recv_sem=rs, device_id=to, device_id_type=MESH
        )

    def plane_peer(k):
        q = lax.rem(place + k, PLANE)
        return device(lax.rem(q, NX), lax.div(q, NX), z, core)

    z_near, z_far = lax.rem(z, NEAR), lax.div(z, NEAR)
    up, down = device(x, y, lax.rem(z + 1, NZ), core), device(x, y, lax.rem(z + NZ - 1, NZ), core)

    def arrived(sem, at):
        remote(at, at, sem, sem, up).wait_recv()

    def gone(sem, at):
        remote(at, at, sem, sem, up).wait_send()

    barrier = pltpu.get_barrier_semaphore()
    greeted = [
        up,
        down,
        device(x, y, z, other),
        device(lax.rem(x + 1, NX), y, z, core),
        device(lax.rem(x + NX - 1, NX), y, z, core),
        device(x, lax.rem(y + 1, NY), z, core),
        device(x, lax.rem(y + NY - 1, NY), z, core),
    ]
    for to in greeted:
        pl.semaphore_signal(barrier, inc=1, device_id=to, device_id_type=MESH)

    MIDDLE = HALF - 1

    def src_start(pos, at_last, c):
        usual = 2 * a * pos
        return pl.multiple_of(usual + at_last * (last + 2 * a - usual) + a * c, UNIT)

    def tgt_start(pos, at_last, c):
        quarter = lax.div(pos + NZ // 4, NZ // 2)
        stored = pos + quarter * (12 - 8 * quarter) * (NZ // 16)
        usual = cols_src + 2 * b * stored
        return pl.multiple_of(usual + at_last * (last - usual) + b * c, UNIT)

    def unit_start(pos, at_last, u):
        if u == 2:
            return tgt_start(pos, at_last, core)
        return pl.multiple_of(src_start(pos, at_last, core) + UNIT * u, UNIT)

    def z_copy(flow, step, u):
        way = 1 - 2 * flow
        at = (flow * HALF + step - 1) * UNITS + u
        before = unit_start(MIDDLE + way * (step - 1), 0, u)
        after = unit_start(MIDDLE + way * step, lax.div(step, HALF), u)
        return remote(
            cols.at[pl.ds(before, UNIT), pl.ds(0, width)],
            cols.at[pl.ds(after, UNIT), pl.ds(0, width)],
            gather_ss.at[0],
            z_rs.at[at],
            up if flow else down,
        )

    def sib_send(step, pos):
        at_last = lax.div(step, HALF)
        sem = lax.div(step + 3, HALF) + at_last
        for start, size in ((src_start(pos, at_last, core), a), (tgt_start(pos, at_last, core), b)):
            at = cols.at[pl.ds(start, size)]
            remote(at, at, gather_ss.at[1], sib_rs.at[sem], device(x, y, z, other)).start()

    def sib_wait(sem, slots):
        arrived(sib_rs.at[sem], cols.at[pl.ds(0, slots * (a + b))])

    def shifted(u, first, second):
        later = lax.div(u * (u - 1), 2)
        f = lax.div((1 - u) * (2 - u), 2) + later * (1 - core)
        xx = lax.rem(x + f * first + (1 - f) * second, NX)
        yy = lax.rem(y + f * second + (1 - f) * first, NY)
        q = yy * NX + xx
        start = (a - (a - b) * later) * q + UNIT * u * (1 - later) + rows_src * later
        return device(xx, yy, z, core), rows.at[pl.ds(pl.multiple_of(start, UNIT), UNIT)]

    def plane_copy(at, sem, to):
        return remote(at, at, gather_ss.at[2], sem, to)

    def first_send(u, k):
        plane_copy(shifted(u, 0, 0)[1], first_rs.at[4 * u + k], shifted(u, k, 0)[0]).start()

    def first_arrival(u, k):
        arrived(first_rs.at[4 * u + k], shifted(u, 4 - k, 0)[1])

    def first_onward(u):
        way = 1 + 2 * lax.rem(u, 2)
        plane_copy(shifted(u, 4 - way, 0)[1], first_rs.at[4 * u + 2], shifted(u, way, 0)[0]).start()

    def second_sends(u, j):
        for k in (1, 3):
            sem = second_rs.at[4 * (4 * u + j) + k]
            plane_copy(shifted(u, 4 - j, 0)[1], sem, shifted(u, 0, k)[0]).start()

    def second_onward(u, j):
        for k in (1, 3):
            arrived(second_rs.at[4 * (4 * u + j) + k], shifted(u, 4 - j, 4 - k)[1])
        way = 1 + 2 * lax.rem(j, 2)
        plane_copy(shifted(u, 4 - j, 4 - way)[1], onward_rs.at[0], shifted(u, 0, way)[0]).start()

    def norm_lanes(source, start, size, targets):
        lane_own = lax.broadcasted_iota(jnp.int32, (size, 128), 1)
        v = source[pl.ds(start, size), 0:width].astype(jnp.float32)
        v = v * v
        total = tree(add, [v[:, 128 * h : 128 * h + 128] for h in range(width // 128)])
        rest = -0.5 * jnp.sum(total, axis=1, keepdims=True)
        terms = []
        for _ in range(3):
            term = rest.astype(jnp.bfloat16).astype(jnp.float32)
            rest = rest - term
            terms.append(term)
        for target, at, first in targets:
            more = jnp.where(lane_own < 6, 1.0, 0.0)
            for k, term in enumerate(terms):
                more = jnp.where(lane_own == first + k, term, more)
            target[pl.ds(at, size), width : width + 128] = more.astype(jnp.bfloat16)

    mine = (
        (src_ref, a, pl.multiple_of(a * place, UNIT), src_start(MIDDLE, 0, core)),
        (tgt_ref, b, pl.multiple_of(rows_src + b * place, UNIT), tgt_start(MIDDLE, 0, core)),
    )
    own_copies = []
    for kind, (ref, size, as_row, as_col) in enumerate(mine):
        for k, (target, at) in enumerate(((rows, as_row), (cols, as_col))):
            own_copies.append(
                pltpu.make_async_copy(
                    ref, target.at[pl.ds(at, size), pl.ds(0, width)], own_sem.at[2 * kind + k]
                )
            )
    for copy in own_copies:
        copy.start()
    row_recv[...] = jnp.ones(row_recv.shape, jnp.float32)
    row_send[...] = jnp.ones(row_send.shape, jnp.float32)
    for copy in own_copies:
        copy.wait()
    pl.semaphore_wait(barrier, len(greeted))

    for u in range(UNITS):
        z_copy(0, 1, u).start()
        z_copy(1, 1, u).start()
    for _, size, as_row, as_col in mine:
        norm_lanes(rows, as_row, size, [(rows, as_row, 0), (cols, as_col, 3)])

    def plane_start(u):
        first_send(u, 1)
        first_send(u, 3)

    each(0, UNITS, plane_start)
    each(0, UNITS, lambda u: second_sends(u, 0))
    sib_send(0, MIDDLE)

    outer_end = cols_src + cols_tgt // 2
    empty = jnp.zeros((2 * a, width + 128), jnp.bfloat16)
    cols[cols_src - 2 * a : cols_src, :] = empty
    cols[outer_end - 2 * b : outer_end, :] = empty[: 2 * b]
    cols[last + 2 * b : last + 2 * a, :] = empty[: 2 * a - 2 * b]

    def product(r, start, size):
        at = pl.ds(pl.multiple_of(r * TILE, TILE), TILE)
        cross = lax.dot_general(
            rows[at, :],
            cols[pl.ds(pl.multiple_of(start, 128), size), :],
            (((1,), (1,)), ((), ())),
            preferred_element_type=jnp.float32,
        )
        return at, [cross[:, 128 * h : 128 * h + 128] * SCALE for h in range(size // 128)]

    def tile(t):
        outer, i = lax.div(t, 7), lax.rem(t, 7)
        is_tgt = lax.div(i, 4)
        r = lax.rem(i, 2) + 2 * lax.div(i, 6)
        g = (1 - outer) * (1 + lax.div(i, 2)) + outer * 3 * lax.div(i, 2)
        at, (one, two) = product(
            r, (1 - is_tgt) * TILE * g + is_tgt * (cols_src + (1 - outer) * (cols_tgt // 2)), TILE
        )
        is_self = (i < 4) | (i == 6)
        lane_one = (1 - is_tgt) * TILE * g + is_tgt * (cols_src + 128 * (1 - outer))
        lane_two = (1 - is_tgt) * (TILE * g + 128) + is_tgt * (cols_src + 256 + 128 * outer)
        for value, lanes in ((one, lane_one), (two, lane_two)):
            scores[at, pl.ds(pl.multiple_of(lanes, 128), 128)] = jnp.where(is_self, jnp.exp2(value), value)

    lane1 = lax.broadcasted_iota(jnp.int32, (1, 128), 1)

    def last_tile(r):
        at, (value,) = product(r, last, 128)
        e = jnp.exp2(value)
        src_lanes, tgt_lanes = slice(cols_src - 128, cols_src), slice(last - 128, last)
        scores[at, src_lanes] = jnp.where(lane1 >= 2 * a, e, scores[at, src_lanes])
        moved = pltpu.roll(jnp.where(r * TILE < rows_src, value, e), 128 - 2 * b, 1)
        scores[at, tgt_lanes] = jnp.where(lane1 >= 128 - 2 * b, moved, scores[at, tgt_lanes])

    def ring_step(step):
        for u in range(UNITS):
            for flow in range(2):
                steps = HALF if flow == (1 if u == 1 else 0) else HALF - 1

                @pl.when(step <= steps)
                def _():
                    z_copy(flow, step, u).wait_recv()

                @pl.when(step < steps)
                def _():
                    z_copy(flow, step + 1, u).start()

        def to_other(flow):
            pos = MIDDLE + (1 - 2 * flow) * step
            at_last = lax.div(step, HALF)
            for start, size in ((src_start(pos, at_last, core), a), (tgt_start(pos, at_last, core), b)):
                norm_lanes(cols, start, size, [(cols, start, 3)])
            sib_send(step, pos)

        each(0, 2 - lax.div(step, HALF), to_other)

        @pl.when(step == 1)
        def _():
            def stage(u):
                first_arrival(u, 1)
                first_arrival(u, 3)
                first_onward(u)
                second_sends(u, 1)
                second_sends(u, 3)

            each(0, UNITS, stage)

        @pl.when(step == 2)
        def _():
            def stage(u):
                first_arrival(u, 2)
                second_sends(u, 2)

            each(0, UNITS, stage)

        @pl.when((step >= 2) & (step <= 4))
        def _():
            def stage(i):
                u, k = lax.rem(i, UNITS), lax.div(i, UNITS)
                second_onward(u, k + lax.div(k, 2) - 2 * lax.div(k, 3))

            each(
                UNITS * (2 * step - 4 - lax.div(step, 3)),
                UNITS * (2 * step - 3 - lax.div(step, 4)),
                stage,
            )

        @pl.when(step == 5)
        def _():
            arrived(onward_rs.at[0], rows.at[pl.ds(0, 4 * UNITS * UNIT)])
            sib_wait(0, 9)

        @pl.when(step == 7)
        def _():
            sib_wait(1, 6)

        @pl.when(step >= 5)
        def _():
            each(lax.div(7 * (step - 5) + 1, 2), lax.div(7 * (step - 4) + 1, 2), tile)

    each(1, HALF + 1, ring_step)
    sib_wait(2, 1)
    each(0, (rows_src + rows_tgt) // TILE, last_tile)

    lane = lax.broadcasted_iota(jnp.int32, (128, 128), 1)
    lane8 = lax.broadcasted_iota(jnp.int32, (8, 128), 1)
    sub8 = lax.broadcasted_iota(jnp.int32, (8, 128), 0)
    sub16 = lax.broadcasted_iota(jnp.int32, (16, 128), 0)
    used_rows = 2 * blocks_src + blocks_tgt
    is_cross = sub16 < blocks_src
    row_log = jnp.where((sub16 >= blocks_src) & (sub16 < 2 * blocks_src), log_src, log_tgt)

    def over_rows(count, body, init):
        return lax.fori_loop(0, count // STEP, lambda r, c: body(pl.multiple_of(r * STEP, STEP), c), init)

    def zeros8(count):
        return tuple(jnp.zeros((8, 128), jnp.float32) for _ in range(count))

    def roll_flat(block, lanes, rows_on):
        rolled = pltpu.roll(block, lanes, 1)
        rolled = jnp.where(lane8 < lanes, pltpu.roll(rolled, 1, 0), rolled)
        return pltpu.roll(rolled, rows_on, 0)

    def turned(earlier, both, chips):
        flat = 2 * a * chips
        earlier = roll_flat(earlier, lax.rem(flat, 128), lax.div(flat, 128))
        flat = 2 * b * chips
        lanes, rows_on = lax.rem(flat, 128), lax.div(flat, 128)
        swapped = pltpu.roll(both, 4, 0)
        cross = roll_flat(jnp.where(sub8 < 4, both, swapped), lanes, rows_on)
        later = roll_flat(jnp.where(sub8 < 4, swapped, both), lanes, rows_on)
        return earlier, jnp.where(sub8 < 4, cross, later)

    chips_on = lax.rem(z + HALF + 1, NZ)

    def merged(parts, logs):
        total = tree(add, parts)
        if logs is None:
            return total
        top = tree(jnp.maximum, parts)
        return jnp.where((sub8 < 4) & logs, top + jnp.log2(tree(add, [jnp.exp2(p - top) for p in parts])), total)

    def lanes_at(h, first=0):
        return slice(first + 128 * h, first + 128 * h + 128)

    col_pot[0] = jnp.ones((8, 128), jnp.float32)
    col_pot[1] = jnp.where(sub8 < 4, 0.0, 1.0)

    def iteration(index):
        def src_rows_part(r):
            at = pl.ds(r, 32)
            values = [scores[at, lanes_at(h, cols_src)] + col_pot[1, h : h + 1] for h in range(lanes_tgt)]
            top = tree(jnp.maximum, values)
            best[at, :] = top
            acc_cross[at, :] = tree(add, [jnp.exp2(v - top) for v in values])
            acc[at, :] = tree(add, [scores[at, lanes_at(h)] * col_pot[0, h : h + 1] for h in range(lanes_src)])

        def tgt_rows_part(r):
            at = pl.ds(rows_src + r, 32)
            acc[at, :] = tree(
                add,
                [scores[at, lanes_at(h, cols_src)] * col_pot[1, 4 + h : 5 + h] for h in range(lanes_tgt)],
            )

        def in_parts(part):
            def body(r, carry):
                for k in range(STEP // 32):
                    part(r + 32 * k)
                return carry

            return body

        over_rows(rows_src, in_parts(src_rows_part), 0)
        over_rows(rows_tgt, in_parts(tgt_rows_part), 0)
        def over_sublanes(block, op, reduce):
            return reduce(fold_rows(block, op), axis=0, keepdims=True)

        for r in range(blocks_src + blocks_tgt):
            at = slice(128 * r, 128 * r + 128)
            if r < blocks_src:
                each_top = best[at, :].T
                top = over_sublanes(each_top, jnp.maximum, jnp.max)
                total = over_sublanes(acc_cross[at, :].T * jnp.exp2(each_top - top), add, jnp.sum)
                row_send[index, r : r + 1] = top + jnp.log2(total)
            row = blocks_src + r
            row_send[index, row : row + 1] = over_sublanes(acc[at, :].T, add, jnp.sum)
        row_recv[index, place] = row_send[index]
        sent = row_send.at[index, pl.ds(0, used_rows)]
        for k in range(1, PLANE):
            remote(
                sent,
                row_recv.at[index, place, pl.ds(0, used_rows)],
                row_ss.at[index],
                row_rs.at[index],
                plane_peer(k),
            ).start()
        others = row_recv.at[index, pl.ds(0, PLANE - 1), pl.ds(0, used_rows)]
        arrived(row_rs.at[index], others)
        parts = [row_recv[index, q] for q in range(PLANE)]
        top = tree(jnp.maximum, parts)
        spread = top + jnp.log2(tree(add, [jnp.exp2(p - top) for p in parts]))
        phi = row_log - jnp.where(is_cross, spread, jnp.log2(tree(add, parts)))
        phi_ref[...] = phi
        table = jnp.where(is_cross, phi, jnp.exp2(phi))
        table = jnp.concatenate([table, jnp.zeros((112, 128), jnp.float32)], axis=0).T
        for r in range(used_rows):
            pot[128 * r : 128 * r + 128, :] = jnp.broadcast_to(table[:, r : r + 1], (128, 128))

        def weighted_cols(first_row, first_col, first_pot, count, lanes):
            def body(r, sums):
                w = pot[pl.ds(first_pot + r, STEP), :]
                return tuple(
                    sums[h] + fold_rows(scores[pl.ds(first_row + r, STEP), lanes_at(h, first_col)] * w, add)
                    for h in range(lanes)
                )

            sums = over_rows(count, body, zeros8(lanes))
            return [jnp.sum(s, axis=0, keepdims=True) for s in sums]

        def cross_body(r, carry):
            w = pot[pl.ds(r, STEP), :]
            out = []
            for h in range(lanes_tgt):
                values = scores[pl.ds(r, STEP), lanes_at(h, cols_src)] + w
                top, total = carry[2 * h], carry[2 * h + 1]
                new_top = jnp.maximum(top, fold_rows(values, jnp.maximum))
                parts = [jnp.exp2(values[8 * k : 8 * k + 8] - new_top) for k in range(STEP // 8)]
                out += [new_top, total * jnp.exp2(top - new_top) + tree(add, parts)]
            return tuple(out)

        start = (jnp.full((8, 128), -1e30, jnp.float32), jnp.zeros((8, 128), jnp.float32))
        sums = over_rows(rows_src, cross_body, start * lanes_tgt)
        tops = [jnp.max(t, axis=0, keepdims=True) for t in sums[::2]]
        sums = [t * jnp.exp2(m - top) for t, m, top in zip(sums[1::2], sums[::2], tops)]
        both = [tops[h] + jnp.log2(jnp.sum(sums[h], axis=0, keepdims=True)) for h in range(lanes_tgt)]
        both = both + weighted_cols(rows_src, cols_src, 2 * rows_src, rows_tgt, lanes_tgt)
        earlier = weighted_cols(0, 0, rows_src, rows_src, lanes_src)
        blocks = turned(jnp.concatenate(earlier, axis=0), jnp.concatenate(both, axis=0), chips_on)
        weight = jnp.where(
            is_cross,
            1.0 / (n_src * SCALE),
            jnp.where(
                sub16 < 2 * blocks_src,
                -0.5 / (n_src * SCALE),
                jnp.where(sub16 < used_rows, -0.5 / (n_tgt * SCALE), 0.0),
            ),
        )
        extra = jnp.sum(phi * weight, axis=0, keepdims=True)

        size = 9
        me_near = 2 * z_near + core
        for k in range(2):
            near_send[index, k, 0:8] = blocks[k]
            near_send[index, k, 8:9] = jnp.zeros_like(extra) if k else extra
        near_recv[index, me_near] = near_send[index, core]

        def near_send_to(o):
            zn, cc = lax.rem(z_near + o // 2, NEAR), lax.rem(core + o % 2, 2)
            remote(
                near_send.at[index, cc, pl.ds(0, size)],
                near_recv.at[index, me_near, pl.ds(0, size)],
                near_ss.at[index],
                near_rs.at[index],
                device(x, y, NEAR * z_far + zn, cc),
            ).start()

        for o in range(1, 2 * NEAR):
            near_send_to(o)
        others = near_recv.at[index, pl.ds(0, 2 * NEAR - 1), pl.ds(0, size)]
        arrived(near_rs.at[index], others)
        me_far = 2 * z_far + core
        block = merged([near_recv[index, q, 0:8] for q in range(2 * NEAR)], core == 1)
        extra = tree(add, [near_recv[index, q, 8:9] for q in range(2 * NEAR)])
        far_send[index, 0:8] = block
        far_send[index, 8:9] = extra
        far_recv[index, me_far, 0:8] = block
        far_recv[index, me_far, 8:9] = extra

        def far_send_to(o):
            zf, cc = lax.rem(z_far + o // 2, FAR), lax.rem(core + o % 2, 2)
            remote(
                far_send.at[index, pl.ds(0, size)],
                far_recv.at[index, me_far, pl.ds(0, size)],
                far_ss.at[index],
                far_rs.at[index],
                device(x, y, NEAR * zf + z_near, cc),
            ).start()

        for o in range(1, 2 * FAR):
            far_send_to(o)
        others = far_recv.at[index, pl.ds(0, 2 * FAR - 1), pl.ds(0, size)]
        arrived(far_rs.at[index], others)
        earlier = merged([far_recv[index, 2 * q, 0:8] for q in range(FAR)], None)
        both = merged([far_recv[index, 2 * q + 1, 0:8] for q in range(FAR)], True)
        totals[0] = earlier
        totals[1] = both
        totals[2, 0:1] = tree(add, [far_recv[index, 2 * q, 8:9] for q in range(FAR)])

        @pl.when(index == 0)
        def _():
            earlier_pot, both_pot = turned(
                n_src / earlier,
                jnp.where(sub8 < 4, log_src - both, n_tgt / both),
                lax.rem(NZ - chips_on, NZ),
            )
            col_pot[0] = earlier_pot
            col_pot[1] = both_pot

    each(0, ITERS, iteration)

    earlier, both = totals[0], totals[1]
    both = (1.0 / SCALE) * jnp.where(sub8 < 4, log_src - both, log_tgt - jnp.log2(both))
    earlier = (1.0 / SCALE) * (log_src - jnp.log2(earlier))
    share = jnp.where(sub8 < 4, 1.0 / n_tgt, -0.5 / n_tgt) * both - (0.5 / n_src) * earlier
    share = jnp.sum(share, axis=0, keepdims=True)

    sum_send[...] = share
    sum_recv[place] = share
    for k in range(1, PLANE):
        remote(sum_send, sum_recv.at[place], sum_ss.at[0], sum_rs.at[0], plane_peer(k)).start()

    def front(block, at, size):
        per = 128 // size
        return pltpu.roll(
            pltpu.roll(block, lax.rem(8 - lax.div(at, per), 8), 0),
            lax.rem(128 - size * lax.rem(at, per), 128),
            1,
        )

    duals = phi_ref[...] * (1.0 / SCALE)
    src_rows = front(duals[0:8], place, a)
    tgt_rows = front(duals[8:16], place, b)
    tgt_cols = front(both, 2 * z + core, b)
    returned = jnp.where(
        sub8 == 1,
        pltpu.roll(src_rows, 5, 0),
        jnp.where(
            sub8 == 2,
            pltpu.roll(tgt_rows, 2, 0),
            jnp.where(sub8 == 3, pltpu.roll(tgt_cols, 3, 0), src_rows),
        ),
    )
    gone(gather_ss.at[0], cols.at[pl.ds(0, UNIT * (2 * HALF - 1) * UNITS), pl.ds(0, width)])
    gone(gather_ss.at[1], cols.at[pl.ds(0, NZ * (a + b))])
    gone(gather_ss.at[2], rows.at[pl.ds(0, UNIT * (PLANE - 1) * UNITS)])
    for index in range(ITERS):
        gone(row_ss.at[index], row_recv.at[index, pl.ds(0, PLANE - 1), pl.ds(0, used_rows)])
        gone(near_ss.at[index], near_recv.at[index, pl.ds(0, 2 * NEAR - 1), pl.ds(0, 9)])
        gone(far_ss.at[index], far_recv.at[index, pl.ds(0, 2 * FAR - 1), pl.ds(0, 9)])
    others = sum_recv.at[pl.ds(0, PLANE - 1)]
    arrived(sum_rs.at[0], others)
    share = totals[2, 0:1] + tree(add, [sum_recv[q] for q in range(PLANE)])
    out_ref[...] = jnp.where(sub8 == 4, jnp.sum(share, axis=1, keepdims=True), returned)
    gone(sum_ss.at[0], others)


def hand_out(block_ref, left_ref, right_ref, earlier_ref, later_ref, div_ref):
    for k, ref in enumerate((left_ref, earlier_ref, later_ref, right_ref, div_ref)):
        ref[...] = block_ref[k : k + 1, 0 : ref.shape[1]]


def per_device(earlier_vectors, later_vectors):
    a, width = earlier_vectors.shape
    b = later_vectors.shape[0]
    rows_src, rows_tgt = a * PLANE, b * PLANE
    cols_src, cols_tgt = 2 * a * NZ, 2 * b * NZ
    rows_all, cols_all = rows_src + rows_tgt, cols_src + cols_tgt
    f32, bf16 = jnp.float32, jnp.bfloat16
    dma = pltpu.SemaphoreType.DMA
    wide = width + 128
    block = pl.pallas_call(
        kernel,
        out_shape=jax.ShapeDtypeStruct((8, 128), f32),
        in_specs=[pl.BlockSpec(memory_space=pltpu.HBM)] * 2,
        out_specs=pl.BlockSpec(memory_space=pltpu.VMEM),
        scratch_shapes=[
            pltpu.VMEM((rows_all, wide), bf16),
            pltpu.VMEM((cols_all + 128, wide), bf16),
            pltpu.VMEM((rows_all, cols_all), f32),
            pltpu.VMEM((rows_src, 128), f32),
            pltpu.VMEM((rows_all, 128), f32),
            pltpu.VMEM((rows_src, 128), f32),
            pltpu.VMEM((2 * rows_src + rows_tgt, 128), f32),
            pltpu.VMEM((2, 8, 128), f32),
            pltpu.VMEM((16, 128), f32),
            pltpu.VMEM((3, 8, 128), f32),
            pltpu.VMEM((ITERS, 16, 128), f32),
            pltpu.VMEM((ITERS, PLANE, 16, 128), f32),
            pltpu.VMEM((ITERS, 2, 16, 128), f32),
            pltpu.VMEM((ITERS, 2 * NEAR, 16, 128), f32),
            pltpu.VMEM((ITERS, 16, 128), f32),
            pltpu.VMEM((ITERS, 2 * FAR, 16, 128), f32),
            pltpu.VMEM((1, 128), f32),
            pltpu.VMEM((PLANE, 1, 128), f32),
            dma((4,)),
            dma((2 * HALF * UNITS,)),
            dma((3,)),
            dma((4 * UNITS,)),
            dma((16 * UNITS,)),
            dma((1,)),
            dma((3,)),
            dma((ITERS,)),
            dma((ITERS,)),
            dma((ITERS,)),
            dma((ITERS,)),
            dma((ITERS,)),
            dma((ITERS,)),
            dma((1,)),
            dma((1,)),
        ],
        compiler_params=pltpu.CompilerParams(
            collective_id=0, has_side_effects=True, vmem_limit_bytes=60 * 1024 * 1024
        ),
        cost_estimate=pl.CostEstimate(
            flops=2 * wide * (rows_src * cols_all + rows_tgt * cols_tgt),
            bytes_accessed=2 * width * (a + b),
            transcendentals=rows_src * (cols_src + 3 * cols_tgt) + rows_tgt * cols_tgt,
        ),
    )(earlier_vectors, later_vectors)
    vmem = pl.BlockSpec(memory_space=pltpu.VMEM)
    left, right, earlier, later, div = pl.pallas_call(
        hand_out,
        out_shape=tuple(jax.ShapeDtypeStruct(s, f32) for s in ((1, a), (1, b), (1, a), (1, b), (1, 1))),
        in_specs=[vmem],
        out_specs=(vmem,) * 5,
    )(block)
    return left.reshape(a), right.reshape(b), earlier.reshape(a), later.reshape(b), div.reshape(())


def solution(mesh):
    return jax.shard_map(
        per_device,
        mesh=mesh,
        in_specs=(P(("row", "col"), None), P(("row", "col"), None)),
        out_specs=(P(("row", "col")), P(("row", "col")), P(("row", "col")), P(("row", "col")), P()),
        check_vma=False,
    )
```

```python
import functools

import jax
import jax.numpy as jnp
import numpy as np
from jax import lax
from jax.experimental import pallas as pl
from jax.experimental.pallas import tpu as pltpu
from jax.sharding import PartitionSpec as P

EPSILON = 0.04
ITERS = 2
MESH = pl.DeviceIdType.MESH

NX, NY, NZ = 4, 4, 16
PLANE = NX * NY
HALF = NZ // 2
NEAR = 4
FAR = NZ // NEAR
UNIT = 16
UNITS = 3
TILE = 256
STEP = 128
SCALE = float(np.log2(np.e)) / EPSILON


def add(a, b):
    return a + b


def tree(op, parts):
    while len(parts) > 1:
        parts = [op(parts[i], parts[i + 1]) for i in range(0, len(parts) - 1, 2)] + (
            [parts[-1]] if len(parts) % 2 else []
        )
    return parts[0]


def fold_rows(x, op):
    return tree(op, [x[8 * k : 8 * k + 8] for k in range(x.shape[0] // 8)])


def quotient(number, by):
    return number // by if isinstance(number, int) else lax.div(number, by)


def multiple(number, of):
    return number if isinstance(number, int) else pl.multiple_of(number, of)


def each(lower, upper, body):
    def step(k, carry):
        body(k)
        return carry

    lax.fori_loop(lower, upper, step, 0)


def kernel(
    src_ref,
    tgt_ref,
    out_ref,
    rows,
    cols,
    scores,
    best,
    acc,
    acc_cross,
    pot,
    col_pot,
    phi_ref,
    totals,
    row_send,
    row_recv,
    near_send,
    near_recv,
    far_send,
    far_recv,
    sum_send,
    sum_recv,
    own_sem,
    z_rs,
    sib_rs,
    first_rs,
    second_rs,
    onward_rs,
    gather_ss,
    row_ss,
    row_rs,
    near_ss,
    near_rs,
    far_ss,
    far_rs,
    sum_ss,
    sum_rs,
):
    a, width = src_ref.shape
    b = tgt_ref.shape[0]
    n_src, n_tgt = a * PLANE * NZ * 2, b * PLANE * NZ * 2
    log_src, log_tgt = float(np.log2(n_src)), float(np.log2(n_tgt))
    rows_src, rows_tgt = a * PLANE, b * PLANE
    cols_src, cols_tgt = a * NZ * 2, b * NZ * 2
    last = cols_src + cols_tgt
    lanes_src, lanes_tgt = cols_src // 128, cols_tgt // 128
    blocks_src, blocks_tgt = rows_src // 128, rows_tgt // 128

    row, col = lax.axis_index("row"), lax.axis_index("col")
    y, z = lax.div(row, NZ), lax.rem(row, NZ)
    x, core = lax.div(col, 2), lax.rem(col, 2)
    other = 1 - core
    place = y * NX + x

    def device(xx, yy, zz, cc):
        return (yy * NZ + zz, xx * 2 + cc)

    def remote(src, dst, ss, rs, to):
        return pltpu.make_async_remote_copy(
            src_ref=src, dst_ref=dst, send_sem=ss, recv_sem=rs, device_id=to, device_id_type=MESH
        )

    def plane_peer(k):
        q = lax.rem(place + k, PLANE)
        return device(lax.rem(q, NX), lax.div(q, NX), z, core)

    z_near, z_far = lax.rem(z, NEAR), lax.div(z, NEAR)
    up, down = device(x, y, lax.rem(z + 1, NZ), core), device(x, y, lax.rem(z + NZ - 1, NZ), core)

    def arrived(sem, at):
        remote(at, at, sem, sem, up).wait_recv()

    def gone(sem, at):
        remote(at, at, sem, sem, up).wait_send()

    barrier = pltpu.get_barrier_semaphore()
    greeted = [
        up,
        down,
        device(x, y, z, other),
        device(lax.rem(x + 1, NX), y, z, core),
        device(lax.rem(x + NX - 1, NX), y, z, core),
        device(x, lax.rem(y + 1, NY), z, core),
        device(x, lax.rem(y + NY - 1, NY), z, core),
    ]
    for to in greeted:
        pl.semaphore_signal(barrier, inc=1, device_id=to, device_id_type=MESH)

    MIDDLE = HALF - 1

    def src_start(pos, at_last, c):
        usual = 2 * a * pos
        return pl.multiple_of(usual + at_last * (last + 2 * a - usual) + a * c, UNIT)

    def tgt_start(pos, at_last, c):
        quarter = lax.div(pos + NZ // 4, NZ // 2)
        stored = pos + quarter * (12 - 8 * quarter) * (NZ // 16)
        usual = cols_src + 2 * b * stored
        return pl.multiple_of(usual + at_last * (last - usual) + b * c, UNIT)

    def unit_start(pos, at_last, u):
        if u == 2:
            return tgt_start(pos, at_last, core)
        return pl.multiple_of(src_start(pos, at_last, core) + UNIT * u, UNIT)

    def z_copy(flow, step, u):
        way = 1 - 2 * flow
        at = (flow * HALF + step - 1) * UNITS + u
        before = unit_start(MIDDLE + way * (step - 1), 0, u)
        after = unit_start(MIDDLE + way * step, lax.div(step, HALF), u)
        return remote(
            cols.at[pl.ds(before, UNIT), pl.ds(0, width)],
            cols.at[pl.ds(after, UNIT), pl.ds(0, width)],
            gather_ss.at[0],
            z_rs.at[at],
            up if flow else down,
        )

    def sib_send(step, pos):
        at_last = lax.div(step, HALF)
        sem = lax.div(step + 3, HALF) + at_last
        for start, size in ((src_start(pos, at_last, core), a), (tgt_start(pos, at_last, core), b)):
            at = cols.at[pl.ds(start, size)]
            remote(at, at, gather_ss.at[1], sib_rs.at[sem], device(x, y, z, other)).start()

    def sib_wait(sem, slots):
        arrived(sib_rs.at[sem], cols.at[pl.ds(0, slots * (a + b))])

    def shifted(u, first, second):
        later = lax.div(u * (u - 1), 2)
        f = lax.div((1 - u) * (2 - u), 2) + later * (1 - core)
        xx = lax.rem(x + f * first + (1 - f) * second, NX)
        yy = lax.rem(y + f * second + (1 - f) * first, NY)
        q = yy * NX + xx
        start = (a - (a - b) * later) * q + UNIT * u * (1 - later) + rows_src * later
        return device(xx, yy, z, core), rows.at[pl.ds(pl.multiple_of(start, UNIT), UNIT)]

    def plane_copy(at, sem, to):
        return remote(at, at, gather_ss.at[2], sem, to)

    def first_send(u, k):
        plane_copy(shifted(u, 0, 0)[1], first_rs.at[4 * u + k], shifted(u, k, 0)[0]).start()

    def first_arrival(u, k):
        arrived(first_rs.at[4 * u + k], shifted(u, 4 - k, 0)[1])

    def first_onward(u):
        way = 1 + 2 * lax.rem(u, 2)
        plane_copy(shifted(u, 4 - way, 0)[1], first_rs.at[4 * u + 2], shifted(u, way, 0)[0]).start()

    def second_sends(u, j):
        for k in (1, 3):
            sem = second_rs.at[4 * (4 * u + j) + k]
            plane_copy(shifted(u, 4 - j, 0)[1], sem, shifted(u, 0, k)[0]).start()

    def second_onward(u, j):
        for k in (1, 3):
            arrived(second_rs.at[4 * (4 * u + j) + k], shifted(u, 4 - j, 4 - k)[1])
        way = 1 + 2 * lax.rem(j, 2)
        plane_copy(shifted(u, 4 - j, 4 - way)[1], onward_rs.at[0], shifted(u, 0, way)[0]).start()

    def norm_lanes(source, start, size, targets):
        lane_own = lax.broadcasted_iota(jnp.int32, (size, 128), 1)
        v = source[pl.ds(start, size), 0:width].astype(jnp.float32)
        v = v * v
        total = tree(add, [v[:, 128 * h : 128 * h + 128] for h in range(width // 128)])
        rest = -0.5 * jnp.sum(total, axis=1, keepdims=True)
        terms = []
        for _ in range(3):
            term = rest.astype(jnp.bfloat16).astype(jnp.float32)
            rest = rest - term
            terms.append(term)
        for target, at, first in targets:
            more = jnp.where(lane_own < 6, 1.0, 0.0)
            for k, term in enumerate(terms):
                more = jnp.where(lane_own == first + k, term, more)
            target[pl.ds(at, size), width : width + 128] = more.astype(jnp.bfloat16)

    mine = (
        (src_ref, a, pl.multiple_of(a * place, UNIT), src_start(MIDDLE, 0, core)),
        (tgt_ref, b, pl.multiple_of(rows_src + b * place, UNIT), tgt_start(MIDDLE, 0, core)),
    )
    own_copies = []
    for kind, (ref, size, as_row, as_col) in enumerate(mine):
        for k, (target, at) in enumerate(((rows, as_row), (cols, as_col))):
            own_copies.append(
                pltpu.make_async_copy(
                    ref, target.at[pl.ds(at, size), pl.ds(0, width)], own_sem.at[2 * kind + k]
                )
            )
    for copy in own_copies:
        copy.start()
    row_recv[...] = jnp.ones(row_recv.shape, jnp.float32)
    row_send[...] = jnp.ones(row_send.shape, jnp.float32)
    for copy in own_copies:
        copy.wait()
    pl.semaphore_wait(barrier, len(greeted))

    for u in range(UNITS):
        z_copy(0, 1, u).start()
        z_copy(1, 1, u).start()
    for _, size, as_row, as_col in mine:
        norm_lanes(rows, as_row, size, [(rows, as_row, 0), (cols, as_col, 3)])

    def plane_start(u):
        first_send(u, 1)
        first_send(u, 3)

    each(0, UNITS, plane_start)
    each(0, UNITS, lambda u: second_sends(u, 0))
    sib_send(0, MIDDLE)

    outer_end = cols_src + cols_tgt // 2
    empty = jnp.zeros((2 * a, width + 128), jnp.bfloat16)
    cols[cols_src - 2 * a : cols_src, :] = empty
    cols[outer_end - 2 * b : outer_end, :] = empty[: 2 * b]
    cols[last + 2 * b : last + 2 * a, :] = empty[: 2 * a - 2 * b]

    def product(r, start, size):
        at = pl.ds(multiple(r * TILE, TILE), TILE)
        cross = lax.dot_general(
            rows[at, :],
            cols[pl.ds(multiple(start, 128), size), :],
            (((1,), (1,)), ((), ())),
            preferred_element_type=jnp.float32,
        )
        return at, [cross[:, 128 * h : 128 * h + 128] * SCALE for h in range(size // 128)]

    def tile(t):
        outer, i = quotient(t, 7), t - 7 * quotient(t, 7)
        is_tgt, pair = quotient(i, 4), quotient(i, 2)
        r = i - 2 * pair + 2 * quotient(i, 6)
        g = (1 - outer) * (1 + pair) + outer * 3 * pair
        at, (one, two) = product(
            r, (1 - is_tgt) * TILE * g + is_tgt * (cols_src + (1 - outer) * (cols_tgt // 2)), TILE
        )
        is_self = (i < 4) | (i == 6)
        lane_one = (1 - is_tgt) * TILE * g + is_tgt * (cols_src + 128 * (1 - outer))
        lane_two = (1 - is_tgt) * (TILE * g + 128) + is_tgt * (cols_src + 256 + 128 * outer)
        for value, lanes in ((one, lane_one), (two, lane_two)):
            if isinstance(t, int):
                value = jnp.exp2(value) if is_self else value
            else:
                value = jnp.where(is_self, jnp.exp2(value), value)
            scores[at, pl.ds(multiple(lanes, 128), 128)] = value

    lane1 = lax.broadcasted_iota(jnp.int32, (1, 128), 1)

    def last_tile(r):
        at, (value,) = product(r, last, 128)
        e = jnp.exp2(value)
        src_lanes, tgt_lanes = slice(cols_src - 128, cols_src), slice(last - 128, last)
        scores[at, src_lanes] = jnp.where(lane1 >= 2 * a, e, scores[at, src_lanes])
        moved = pltpu.roll(value if r * TILE < rows_src else e, 128 - 2 * b, 1)
        scores[at, tgt_lanes] = jnp.where(lane1 >= 128 - 2 * b, moved, scores[at, tgt_lanes])

    def ring_step(step):
        for u in range(UNITS):
            for flow in range(2):
                longer = 1 if flow == (1 if u == 1 else 0) else 0
                steps = HALF - 1 + longer + core * (1 - 2 * longer)

                @pl.when(step <= steps)
                def _():
                    z_copy(flow, step, u).wait_recv()

                @pl.when(step < steps)
                def _():
                    z_copy(flow, step + 1, u).start()

        def to_other(flow):
            pos = MIDDLE + (1 - 2 * flow) * step
            at_last = lax.div(step, HALF)
            for start, size in ((src_start(pos, at_last, core), a), (tgt_start(pos, at_last, core), b)):
                norm_lanes(cols, start, size, [(cols, start, 3)])
            sib_send(step, pos)

        each(0, 2 - lax.div(step, HALF), to_other)

        @pl.when(step == 1)
        def _():
            def stage(u):
                first_arrival(u, 1)
                first_arrival(u, 3)
                first_onward(u)
                second_sends(u, 1)
                second_sends(u, 3)

            each(0, UNITS, stage)

        @pl.when(step == 2)
        def _():
            def stage(u):
                first_arrival(u, 2)
                second_sends(u, 2)

            each(0, UNITS, stage)

        @pl.when((step >= 2) & (step <= 4))
        def _():
            def stage(i):
                u, k = lax.rem(i, UNITS), lax.div(i, UNITS)
                second_onward(u, k + lax.div(k, 2) - 2 * lax.div(k, 3))

            each(
                UNITS * (2 * step - 4 - lax.div(step, 3)),
                UNITS * (2 * step - 3 - lax.div(step, 4)),
                stage,
            )

        @pl.when(step == 5)
        def _():
            arrived(onward_rs.at[0], rows.at[pl.ds(0, 4 * UNITS * UNIT)])
            sib_wait(0, 9)

        @pl.when(step == 7)
        def _():
            sib_wait(1, 6)

        @pl.when((step >= 5) & (step < HALF))
        def _():
            each(lax.div(7 * (step - 5) + 1, 2), lax.div(7 * (step - 4) + 1, 2), tile)

    each(1, HALF + 1, ring_step)
    for t in (11, 12, 13):
        tile(t)
    sib_wait(2, 1)
    for r in range((rows_src + rows_tgt) // TILE):
        last_tile(r)

    lane = lax.broadcasted_iota(jnp.int32, (128, 128), 1)
    lane8 = lax.broadcasted_iota(jnp.int32, (8, 128), 1)
    sub8 = lax.broadcasted_iota(jnp.int32, (8, 128), 0)
    sub16 = lax.broadcasted_iota(jnp.int32, (16, 128), 0)
    used_rows = 2 * blocks_src + blocks_tgt
    is_cross = sub16 < blocks_src
    row_log = jnp.where((sub16 >= blocks_src) & (sub16 < 2 * blocks_src), log_src, log_tgt)

    def over_rows(count, body, init):
        return lax.fori_loop(0, count // STEP, lambda r, c: body(pl.multiple_of(r * STEP, STEP), c), init)

    def zeros8(count):
        return tuple(jnp.zeros((8, 128), jnp.float32) for _ in range(count))

    def roll_flat(block, lanes, rows_on):
        rolled = pltpu.roll(block, lanes, 1)
        rolled = jnp.where(lane8 < lanes, pltpu.roll(rolled, 1, 0), rolled)
        return pltpu.roll(rolled, rows_on, 0)

    def turned(earlier, both, chips):
        flat = 2 * a * chips
        earlier = roll_flat(earlier, lax.rem(flat, 128), lax.div(flat, 128))
        flat = 2 * b * chips
        lanes, rows_on = lax.rem(flat, 128), lax.div(flat, 128)
        swapped = pltpu.roll(both, 4, 0)
        cross = roll_flat(jnp.where(sub8 < 4, both, swapped), lanes, rows_on)
        later = roll_flat(jnp.where(sub8 < 4, swapped, both), lanes, rows_on)
        return earlier, jnp.where(sub8 < 4, cross, later)

    chips_on = lax.rem(z + HALF + 1, NZ)

    def merged(parts, logs):
        total = tree(add, parts)
        if logs is None:
            return total
        top = tree(jnp.maximum, parts)
        return jnp.where((sub8 < 4) & logs, top + jnp.log2(tree(add, [jnp.exp2(p - top) for p in parts])), total)

    def lanes_at(h, first=0):
        return slice(first + 128 * h, first + 128 * h + 128)

    col_pot[0] = jnp.ones((8, 128), jnp.float32)
    col_pot[1] = jnp.where(sub8 < 4, 0.0, 1.0)

    def iteration(index):
        def src_rows_part(r):
            at = pl.ds(r, 32)
            values = [scores[at, lanes_at(h, cols_src)] + col_pot[1, h : h + 1] for h in range(lanes_tgt)]
            top = tree(jnp.maximum, values)
            best[at, :] = top
            acc_cross[at, :] = tree(add, [jnp.exp2(v - top) for v in values])
            acc[at, :] = tree(add, [scores[at, lanes_at(h)] * col_pot[0, h : h + 1] for h in range(lanes_src)])

        def tgt_rows_part(r):
            at = pl.ds(rows_src + r, 32)
            acc[at, :] = tree(
                add,
                [scores[at, lanes_at(h, cols_src)] * col_pot[1, 4 + h : 5 + h] for h in range(lanes_tgt)],
            )

        def in_parts(part):
            def body(r, carry):
                for k in range(STEP // 32):
                    part(r + 32 * k)
                return carry

            return body

        over_rows(rows_src, in_parts(src_rows_part), 0)
        over_rows(rows_tgt, in_parts(tgt_rows_part), 0)
        def over_sublanes(block, op, reduce):
            return reduce(fold_rows(block, op), axis=0, keepdims=True)

        for r in range(blocks_src + blocks_tgt):
            at = slice(128 * r, 128 * r + 128)
            if r < blocks_src:
                each_top = best[at, :].T
                top = over_sublanes(each_top, jnp.maximum, jnp.max)
                total = over_sublanes(acc_cross[at, :].T * jnp.exp2(each_top - top), add, jnp.sum)
                row_send[index, r : r + 1] = top + jnp.log2(total)
            row = blocks_src + r
            row_send[index, row : row + 1] = over_sublanes(acc[at, :].T, add, jnp.sum)
        row_recv[index, place] = row_send[index]
        sent = row_send.at[index, pl.ds(0, used_rows)]
        for k in range(1, PLANE):
            remote(
                sent,
                row_recv.at[index, place, pl.ds(0, used_rows)],
                row_ss.at[index],
                row_rs.at[index],
                plane_peer(k),
            ).start()
        others = row_recv.at[index, pl.ds(0, PLANE - 1), pl.ds(0, used_rows)]
        arrived(row_rs.at[index], others)
        parts = [row_recv[index, q] for q in range(PLANE)]
        top = tree(jnp.maximum, parts)
        spread = top + jnp.log2(tree(add, [jnp.exp2(p - top) for p in parts]))
        phi = row_log - jnp.where(is_cross, spread, jnp.log2(tree(add, parts)))
        phi_ref[...] = phi
        table = jnp.where(is_cross, phi, jnp.exp2(phi))
        table = jnp.concatenate([table, jnp.zeros((112, 128), jnp.float32)], axis=0).T
        for r in range(used_rows):
            pot[128 * r : 128 * r + 128, :] = jnp.broadcast_to(table[:, r : r + 1], (128, 128))

        def weighted_cols(first_row, first_col, first_pot, count, lanes):
            def body(r, sums):
                w = pot[pl.ds(first_pot + r, STEP), :]
                return tuple(
                    sums[h] + fold_rows(scores[pl.ds(first_row + r, STEP), lanes_at(h, first_col)] * w, add)
                    for h in range(lanes)
                )

            sums = over_rows(count, body, zeros8(lanes))
            return [jnp.sum(s, axis=0, keepdims=True) for s in sums]

        def cross_body(r, carry):
            w = pot[pl.ds(r, STEP), :]
            out = []
            for h in range(lanes_tgt):
                values = scores[pl.ds(r, STEP), lanes_at(h, cols_src)] + w
                top, total = carry[2 * h], carry[2 * h + 1]
                new_top = jnp.maximum(top, fold_rows(values, jnp.maximum))
                parts = [jnp.exp2(values[8 * k : 8 * k + 8] - new_top) for k in range(STEP // 8)]
                out += [new_top, total * jnp.exp2(top - new_top) + tree(add, parts)]
            return tuple(out)

        start = (jnp.full((8, 128), -1e30, jnp.float32), jnp.zeros((8, 128), jnp.float32))
        sums = over_rows(rows_src, cross_body, start * lanes_tgt)
        tops = [jnp.max(t, axis=0, keepdims=True) for t in sums[::2]]
        sums = [t * jnp.exp2(m - top) for t, m, top in zip(sums[1::2], sums[::2], tops)]
        both = [tops[h] + jnp.log2(jnp.sum(sums[h], axis=0, keepdims=True)) for h in range(lanes_tgt)]
        both = both + weighted_cols(rows_src, cols_src, 2 * rows_src, rows_tgt, lanes_tgt)
        earlier = weighted_cols(0, 0, rows_src, rows_src, lanes_src)
        blocks = turned(jnp.concatenate(earlier, axis=0), jnp.concatenate(both, axis=0), chips_on)
        weight = jnp.where(
            is_cross,
            1.0 / (n_src * SCALE),
            jnp.where(
                sub16 < 2 * blocks_src,
                -0.5 / (n_src * SCALE),
                jnp.where(sub16 < used_rows, -0.5 / (n_tgt * SCALE), 0.0),
            ),
        )
        extra = jnp.sum(phi * weight, axis=0, keepdims=True)

        size = 9
        me_near = 2 * z_near + core
        for k in range(2):
            near_send[index, k, 0:8] = blocks[k]
            near_send[index, k, 8:9] = jnp.zeros_like(extra) if k else extra
        near_recv[index, me_near] = near_send[index, core]

        def near_send_to(o):
            zn, cc = lax.rem(z_near + o // 2, NEAR), lax.rem(core + o % 2, 2)
            remote(
                near_send.at[index, cc, pl.ds(0, size)],
                near_recv.at[index, me_near, pl.ds(0, size)],
                near_ss.at[index],
                near_rs.at[index],
                device(x, y, NEAR * z_far + zn, cc),
            ).start()

        for o in range(1, 2 * NEAR):
            near_send_to(o)
        others = near_recv.at[index, pl.ds(0, 2 * NEAR - 1), pl.ds(0, size)]
        arrived(near_rs.at[index], others)
        me_far = 2 * z_far + core
        block = merged([near_recv[index, q, 0:8] for q in range(2 * NEAR)], core == 1)
        extra = tree(add, [near_recv[index, q, 8:9] for q in range(2 * NEAR)])
        far_send[index, 0:8] = block
        far_send[index, 8:9] = extra
        far_recv[index, me_far, 0:8] = block
        far_recv[index, me_far, 8:9] = extra

        def far_send_to(o):
            zf, cc = lax.rem(z_far + o // 2, FAR), lax.rem(core + o % 2, 2)
            remote(
                far_send.at[index, pl.ds(0, size)],
                far_recv.at[index, me_far, pl.ds(0, size)],
                far_ss.at[index],
                far_rs.at[index],
                device(x, y, NEAR * zf + z_near, cc),
            ).start()

        for o in range(1, 2 * FAR):
            far_send_to(o)
        others = far_recv.at[index, pl.ds(0, 2 * FAR - 1), pl.ds(0, size)]
        arrived(far_rs.at[index], others)
        earlier = merged([far_recv[index, 2 * q, 0:8] for q in range(FAR)], None)
        both = merged([far_recv[index, 2 * q + 1, 0:8] for q in range(FAR)], True)
        totals[0] = earlier
        totals[1] = both
        totals[2, 0:1] = tree(add, [far_recv[index, 2 * q, 8:9] for q in range(FAR)])

        @pl.when(index == 0)
        def _():
            earlier_pot, both_pot = turned(
                n_src / earlier,
                jnp.where(sub8 < 4, log_src - both, n_tgt / both),
                lax.rem(NZ - chips_on, NZ),
            )
            col_pot[0] = earlier_pot
            col_pot[1] = both_pot

    each(0, ITERS, iteration)

    earlier, both = totals[0], totals[1]
    both = (1.0 / SCALE) * jnp.where(sub8 < 4, log_src - both, log_tgt - jnp.log2(both))
    earlier = (1.0 / SCALE) * (log_src - jnp.log2(earlier))
    share = jnp.where(sub8 < 4, 1.0 / n_tgt, -0.5 / n_tgt) * both - (0.5 / n_src) * earlier
    share = jnp.sum(share, axis=0, keepdims=True)

    sum_send[...] = share
    sum_recv[place] = share
    for k in range(1, PLANE):
        remote(sum_send, sum_recv.at[place], sum_ss.at[0], sum_rs.at[0], plane_peer(k)).start()

    def front(block, at, size):
        per = 128 // size
        return pltpu.roll(
            pltpu.roll(block, lax.rem(8 - lax.div(at, per), 8), 0),
            lax.rem(128 - size * lax.rem(at, per), 128),
            1,
        )

    duals = phi_ref[...] * (1.0 / SCALE)
    src_rows = front(duals[0:8], place, a)
    tgt_rows = front(duals[8:16], place, b)
    tgt_cols = front(both, 2 * z + core, b)
    returned = jnp.where(
        sub8 == 1,
        pltpu.roll(src_rows, 5, 0),
        jnp.where(
            sub8 == 2,
            pltpu.roll(tgt_rows, 2, 0),
            jnp.where(sub8 == 3, pltpu.roll(tgt_cols, 3, 0), src_rows),
        ),
    )
    gone(gather_ss.at[0], cols.at[pl.ds(0, UNIT * (2 * HALF - 1) * UNITS), pl.ds(0, width)])
    gone(gather_ss.at[1], cols.at[pl.ds(0, NZ * (a + b))])
    gone(gather_ss.at[2], rows.at[pl.ds(0, UNIT * (PLANE - 1) * UNITS)])
    for index in range(ITERS):
        gone(row_ss.at[index], row_recv.at[index, pl.ds(0, PLANE - 1), pl.ds(0, used_rows)])
        gone(near_ss.at[index], near_recv.at[index, pl.ds(0, 2 * NEAR - 1), pl.ds(0, 9)])
        gone(far_ss.at[index], far_recv.at[index, pl.ds(0, 2 * FAR - 1), pl.ds(0, 9)])
    others = sum_recv.at[pl.ds(0, PLANE - 1)]
    arrived(sum_rs.at[0], others)
    share = totals[2, 0:1] + tree(add, [sum_recv[q] for q in range(PLANE)])
    out_ref[...] = jnp.where(sub8 == 4, jnp.sum(share, axis=1, keepdims=True), returned)
    gone(sum_ss.at[0], others)


def hand_out(block_ref, left_ref, right_ref, earlier_ref, later_ref, div_ref):
    for k, ref in enumerate((left_ref, earlier_ref, later_ref, right_ref, div_ref)):
        ref[...] = block_ref[k : k + 1, 0 : ref.shape[1]]


def per_device(earlier_vectors, later_vectors):
    a, width = earlier_vectors.shape
    b = later_vectors.shape[0]
    rows_src, rows_tgt = a * PLANE, b * PLANE
    cols_src, cols_tgt = 2 * a * NZ, 2 * b * NZ
    rows_all, cols_all = rows_src + rows_tgt, cols_src + cols_tgt
    f32, bf16 = jnp.float32, jnp.bfloat16
    dma = pltpu.SemaphoreType.DMA
    wide = width + 128
    block = pl.pallas_call(
        kernel,
        out_shape=jax.ShapeDtypeStruct((8, 128), f32),
        in_specs=[pl.BlockSpec(memory_space=pltpu.HBM)] * 2,
        out_specs=pl.BlockSpec(memory_space=pltpu.VMEM),
        scratch_shapes=[
            pltpu.VMEM((rows_all, wide), bf16),
            pltpu.VMEM((cols_all + 128, wide), bf16),
            pltpu.VMEM((rows_all, cols_all), f32),
            pltpu.VMEM((rows_src, 128), f32),
            pltpu.VMEM((rows_all, 128), f32),
            pltpu.VMEM((rows_src, 128), f32),
            pltpu.VMEM((2 * rows_src + rows_tgt, 128), f32),
            pltpu.VMEM((2, 8, 128), f32),
            pltpu.VMEM((16, 128), f32),
            pltpu.VMEM((3, 8, 128), f32),
            pltpu.VMEM((ITERS, 16, 128), f32),
            pltpu.VMEM((ITERS, PLANE, 16, 128), f32),
            pltpu.VMEM((ITERS, 2, 16, 128), f32),
            pltpu.VMEM((ITERS, 2 * NEAR, 16, 128), f32),
            pltpu.VMEM((ITERS, 16, 128), f32),
            pltpu.VMEM((ITERS, 2 * FAR, 16, 128), f32),
            pltpu.VMEM((1, 128), f32),
            pltpu.VMEM((PLANE, 1, 128), f32),
            dma((4,)),
            dma((2 * HALF * UNITS,)),
            dma((3,)),
            dma((4 * UNITS,)),
            dma((16 * UNITS,)),
            dma((1,)),
            dma((3,)),
            dma((ITERS,)),
            dma((ITERS,)),
            dma((ITERS,)),
            dma((ITERS,)),
            dma((ITERS,)),
            dma((ITERS,)),
            dma((1,)),
            dma((1,)),
        ],
        compiler_params=pltpu.CompilerParams(
            collective_id=0, has_side_effects=True, vmem_limit_bytes=60 * 1024 * 1024
        ),
        cost_estimate=pl.CostEstimate(
            flops=2 * wide * (rows_src * cols_all + rows_tgt * cols_tgt),
            bytes_accessed=2 * width * (a + b),
            transcendentals=rows_src * (cols_src + 3 * cols_tgt) + rows_tgt * cols_tgt,
        ),
    )(earlier_vectors, later_vectors)
    vmem = pl.BlockSpec(memory_space=pltpu.VMEM)
    left, right, earlier, later, div = pl.pallas_call(
        hand_out,
        out_shape=tuple(jax.ShapeDtypeStruct(s, f32) for s in ((1, a), (1, b), (1, a), (1, b), (1, 1))),
        in_specs=[vmem],
        out_specs=(vmem,) * 5,
    )(block)
    return left.reshape(a), right.reshape(b), earlier.reshape(a), later.reshape(b), div.reshape(())


def solution(mesh):
    return jax.shard_map(
        per_device,
        mesh=mesh,
        in_specs=(P(("row", "col"), None), P(("row", "col"), None)),
        out_specs=(P(("row", "col")), P(("row", "col")), P(("row", "col")), P(("row", "col")), P()),
        check_vma=False,
    )
```

```python
import functools

import jax
import jax.numpy as jnp
import numpy as np
from jax import lax
from jax.experimental import pallas as pl
from jax.experimental.pallas import tpu as pltpu
from jax.sharding import PartitionSpec as P

EPSILON = 0.04
ITERS = 2
MESH = pl.DeviceIdType.MESH

NX, NY, NZ = 4, 4, 16
PLANE = NX * NY
HALF = NZ // 2
NEAR = 4
FAR = NZ // NEAR
UNIT = 16
UNITS = 3
TILE = 256
STEP = 128
SCALE = float(np.log2(np.e)) / EPSILON


def add(a, b):
    return a + b


def tree(op, parts):
    while len(parts) > 1:
        parts = [op(parts[i], parts[i + 1]) for i in range(0, len(parts) - 1, 2)] + (
            [parts[-1]] if len(parts) % 2 else []
        )
    return parts[0]


def fold_rows(x, op):
    return tree(op, [x[8 * k : 8 * k + 8] for k in range(x.shape[0] // 8)])


def quotient(number, by):
    return number // by if isinstance(number, int) else lax.div(number, by)


def multiple(number, of):
    return number if isinstance(number, int) else pl.multiple_of(number, of)


def each(lower, upper, body):
    def step(k, carry):
        body(k)
        return carry

    lax.fori_loop(lower, upper, step, 0)


def kernel(
    src_ref,
    tgt_ref,
    out_ref,
    rows,
    cols,
    scores,
    best,
    acc,
    acc_cross,
    pot,
    col_pot,
    phi_ref,
    totals,
    row_send,
    row_recv,
    near_send,
    near_recv,
    far_send,
    far_recv,
    sum_send,
    sum_recv,
    own_sem,
    z_rs,
    sib_rs,
    first_rs,
    second_rs,
    onward_rs,
    gather_ss,
    row_ss,
    row_rs,
    near_ss,
    near_rs,
    far_ss,
    far_rs,
    sum_ss,
    sum_rs,
):
    a, width = src_ref.shape
    b = tgt_ref.shape[0]
    n_src, n_tgt = a * PLANE * NZ * 2, b * PLANE * NZ * 2
    log_src, log_tgt = float(np.log2(n_src)), float(np.log2(n_tgt))
    rows_src, rows_tgt = a * PLANE, b * PLANE
    cols_src, cols_tgt = a * NZ * 2, b * NZ * 2
    last = cols_src + cols_tgt
    lanes_src, lanes_tgt = cols_src // 128, cols_tgt // 128
    blocks_src, blocks_tgt = rows_src // 128, rows_tgt // 128

    row, col = lax.axis_index("row"), lax.axis_index("col")
    y, z = lax.div(row, NZ), lax.rem(row, NZ)
    x, core = lax.div(col, 2), lax.rem(col, 2)
    other = 1 - core
    place = y * NX + x

    def device(xx, yy, zz, cc):
        return (yy * NZ + zz, xx * 2 + cc)

    def remote(src, dst, ss, rs, to):
        return pltpu.make_async_remote_copy(
            src_ref=src, dst_ref=dst, send_sem=ss, recv_sem=rs, device_id=to, device_id_type=MESH
        )

    def plane_peer(k):
        q = lax.rem(place + k, PLANE)
        return device(lax.rem(q, NX), lax.div(q, NX), z, core)

    z_near, z_far = lax.rem(z, NEAR), lax.div(z, NEAR)
    up, down = device(x, y, lax.rem(z + 1, NZ), core), device(x, y, lax.rem(z + NZ - 1, NZ), core)

    def arrived(sem, at):
        remote(at, at, sem, sem, up).wait_recv()

    def gone(sem, at):
        remote(at, at, sem, sem, up).wait_send()

    barrier = pltpu.get_barrier_semaphore()
    greeted = [
        up,
        down,
        device(x, y, z, other),
        device(lax.rem(x + 1, NX), y, z, core),
        device(lax.rem(x + NX - 1, NX), y, z, core),
        device(x, lax.rem(y + 1, NY), z, core),
        device(x, lax.rem(y + NY - 1, NY), z, core),
    ]
    for to in greeted:
        pl.semaphore_signal(barrier, inc=1, device_id=to, device_id_type=MESH)

    MIDDLE = HALF - 1

    def src_start(pos, at_last, c):
        usual = 2 * a * pos
        return pl.multiple_of(usual + at_last * (last + 2 * a - usual) + a * c, UNIT)

    def tgt_start(pos, at_last, c):
        quarter = lax.div(pos + NZ // 4, NZ // 2)
        stored = pos + quarter * (12 - 8 * quarter) * (NZ // 16)
        usual = cols_src + 2 * b * stored
        return pl.multiple_of(usual + at_last * (last - usual) + b * c, UNIT)

    def unit_start(pos, at_last, u):
        if u == 2:
            return tgt_start(pos, at_last, core)
        return pl.multiple_of(src_start(pos, at_last, core) + UNIT * u, UNIT)

    def z_copy(flow, step, u):
        way = 1 - 2 * flow
        at = (flow * HALF + step - 1) * UNITS + u
        before = unit_start(MIDDLE + way * (step - 1), 0, u)
        after = unit_start(MIDDLE + way * step, lax.div(step, HALF), u)
        return remote(
            cols.at[pl.ds(before, UNIT), pl.ds(0, width)],
            cols.at[pl.ds(after, UNIT), pl.ds(0, width)],
            gather_ss.at[0],
            z_rs.at[at],
            up if flow else down,
        )

    def sib_send(step, pos):
        at_last = lax.div(step, HALF)
        sem = lax.div(step + 3, HALF) + at_last
        for start, size in ((src_start(pos, at_last, core), a), (tgt_start(pos, at_last, core), b)):
            at = cols.at[pl.ds(start, size)]
            remote(at, at, gather_ss.at[1], sib_rs.at[sem], device(x, y, z, other)).start()

    def sib_wait(sem, slots):
        arrived(sib_rs.at[sem], cols.at[pl.ds(0, slots * (a + b))])

    def shifted(u, first, second):
        later = lax.div(u * (u - 1), 2)
        f = lax.div((1 - u) * (2 - u), 2) + later * (1 - core)
        xx = lax.rem(x + f * first + (1 - f) * second, NX)
        yy = lax.rem(y + f * second + (1 - f) * first, NY)
        q = yy * NX + xx
        start = (a - (a - b) * later) * q + UNIT * u * (1 - later) + rows_src * later
        return device(xx, yy, z, core), rows.at[pl.ds(pl.multiple_of(start, UNIT), UNIT)]

    def plane_copy(at, sem, to):
        return remote(at, at, gather_ss.at[2], sem, to)

    def first_send(u, k):
        plane_copy(shifted(u, 0, 0)[1], first_rs.at[4 * u + k], shifted(u, k, 0)[0]).start()

    def first_arrival(u, k):
        arrived(first_rs.at[4 * u + k], shifted(u, 4 - k, 0)[1])

    def first_onward(u):
        way = 1 + 2 * lax.rem(u, 2)
        plane_copy(shifted(u, 4 - way, 0)[1], first_rs.at[4 * u + 2], shifted(u, way, 0)[0]).start()

    def second_sends(u, j):
        for k in (1, 3):
            sem = second_rs.at[4 * (4 * u + j) + k]
            plane_copy(shifted(u, 4 - j, 0)[1], sem, shifted(u, 0, k)[0]).start()

    def second_onward(u, j):
        for k in (1, 3):
            arrived(second_rs.at[4 * (4 * u + j) + k], shifted(u, 4 - j, 4 - k)[1])
        way = 1 + 2 * lax.rem(j, 2)
        plane_copy(shifted(u, 4 - j, 4 - way)[1], onward_rs.at[0], shifted(u, 0, way)[0]).start()

    def norm_lanes(source, start, size, targets):
        lane_own = lax.broadcasted_iota(jnp.int32, (size, 128), 1)
        v = source[pl.ds(start, size), 0:width].astype(jnp.float32)
        v = v * v
        total = tree(add, [v[:, 128 * h : 128 * h + 128] for h in range(width // 128)])
        rest = -0.5 * jnp.sum(total, axis=1, keepdims=True)
        terms = []
        for _ in range(3):
            term = rest.astype(jnp.bfloat16).astype(jnp.float32)
            rest = rest - term
            terms.append(term)
        for target, at, first in targets:
            more = jnp.where(lane_own < 6, 1.0, 0.0)
            for k, term in enumerate(terms):
                more = jnp.where(lane_own == first + k, term, more)
            target[pl.ds(at, size), width : width + 128] = more.astype(jnp.bfloat16)

    mine = (
        (src_ref, a, pl.multiple_of(a * place, UNIT), src_start(MIDDLE, 0, core)),
        (tgt_ref, b, pl.multiple_of(rows_src + b * place, UNIT), tgt_start(MIDDLE, 0, core)),
    )
    own_copies = []
    for kind, (ref, size, as_row, as_col) in enumerate(mine):
        for k, (target, at) in enumerate(((rows, as_row), (cols, as_col))):
            own_copies.append(
                pltpu.make_async_copy(
                    ref, target.at[pl.ds(at, size), pl.ds(0, width)], own_sem.at[2 * kind + k]
                )
            )
    for copy in own_copies:
        copy.start()
    row_recv[...] = jnp.ones(row_recv.shape, jnp.float32)
    row_send[...] = jnp.ones(row_send.shape, jnp.float32)
    for copy in own_copies:
        copy.wait()
    pl.semaphore_wait(barrier, len(greeted))

    for u in range(UNITS):
        z_copy(0, 1, u).start()
        z_copy(1, 1, u).start()
    for _, size, as_row, as_col in mine:
        norm_lanes(rows, as_row, size, [(rows, as_row, 0), (cols, as_col, 3)])

    def plane_start(u):
        first_send(u, 1)
        first_send(u, 3)

    each(0, UNITS, plane_start)
    each(0, UNITS, lambda u: second_sends(u, 0))
    sib_send(0, MIDDLE)

    outer_end = cols_src + cols_tgt // 2
    empty = jnp.zeros((2 * a, width + 128), jnp.bfloat16)
    cols[cols_src - 2 * a : cols_src, :] = empty
    cols[outer_end - 2 * b : outer_end, :] = empty[: 2 * b]
    cols[last + 2 * b : last + 2 * a, :] = empty[: 2 * a - 2 * b]

    def product(r, start, size):
        at = pl.ds(multiple(r * TILE, TILE), TILE)
        cross = lax.dot_general(
            rows[at, :],
            cols[pl.ds(multiple(start, 128), size), :],
            (((1,), (1,)), ((), ())),
            preferred_element_type=jnp.float32,
        )
        return at, [cross[:, 128 * h : 128 * h + 128] * SCALE for h in range(size // 128)]

    def tile(t):
        outer, i = quotient(t, 7), t - 7 * quotient(t, 7)
        is_tgt, pair = quotient(i, 4), quotient(i, 2)
        r = i - 2 * pair + 2 * quotient(i, 6)
        g = (1 - outer) * (1 + pair) + outer * 3 * pair
        at, (one, two) = product(
            r, (1 - is_tgt) * TILE * g + is_tgt * (cols_src + (1 - outer) * (cols_tgt // 2)), TILE
        )
        is_self = (i < 4) | (i == 6)
        lane_one = (1 - is_tgt) * TILE * g + is_tgt * (cols_src + 128 * (1 - outer))
        lane_two = (1 - is_tgt) * (TILE * g + 128) + is_tgt * (cols_src + 256 + 128 * outer)
        for value, lanes in ((one, lane_one), (two, lane_two)):
            if isinstance(t, int):
                value = jnp.exp2(value) if is_self else value
            else:
                value = jnp.where(is_self, jnp.exp2(value), value)
            scores[at, pl.ds(multiple(lanes, 128), 128)] = value

    lane1 = lax.broadcasted_iota(jnp.int32, (1, 128), 1)

    def last_tile(r):
        at, (value,) = product(r, last, 128)
        e = jnp.exp2(value)
        src_lanes, tgt_lanes = slice(cols_src - 128, cols_src), slice(last - 128, last)
        scores[at, src_lanes] = jnp.where(lane1 >= 2 * a, e, scores[at, src_lanes])
        moved = pltpu.roll(value if r * TILE < rows_src else e, 128 - 2 * b, 1)
        scores[at, tgt_lanes] = jnp.where(lane1 >= 128 - 2 * b, moved, scores[at, tgt_lanes])

    def ring_step(step):
        for u in range(UNITS):
            for flow in range(2):
                longer = 1 if flow == (1 if u == 1 else 0) else 0
                steps = HALF - 1 + longer + core * (1 - 2 * longer)

                @pl.when(step <= steps)
                def _():
                    z_copy(flow, step, u).wait_recv()

                @pl.when(step < steps)
                def _():
                    z_copy(flow, step + 1, u).start()

        def to_other(flow):
            pos = MIDDLE + (1 - 2 * flow) * step
            at_last = lax.div(step, HALF)
            for start, size in ((src_start(pos, at_last, core), a), (tgt_start(pos, at_last, core), b)):
                norm_lanes(cols, start, size, [(cols, start, 3)])
            sib_send(step, pos)

        each(0, 2 - lax.div(step, HALF), to_other)

        @pl.when(step == 1)
        def _():
            def stage(u):
                first_arrival(u, 1)
                first_arrival(u, 3)
                first_onward(u)
                second_sends(u, 1)
                second_sends(u, 3)

            each(0, UNITS, stage)

        @pl.when(step == 2)
        def _():
            def stage(u):
                first_arrival(u, 2)
                second_sends(u, 2)

            each(0, UNITS, stage)

        @pl.when((step >= 2) & (step <= 4))
        def _():
            def stage(i):
                u, k = lax.rem(i, UNITS), lax.div(i, UNITS)
                second_onward(u, k + lax.div(k, 2) - 2 * lax.div(k, 3))

            each(
                UNITS * (2 * step - 4 - lax.div(step, 3)),
                UNITS * (2 * step - 3 - lax.div(step, 4)),
                stage,
            )

        @pl.when(step == 5)
        def _():
            arrived(onward_rs.at[0], rows.at[pl.ds(0, 4 * UNITS * UNIT)])
            sib_wait(0, 9)

        @pl.when(step == 7)
        def _():
            sib_wait(1, 6)

        @pl.when((step >= 5) & (step < HALF))
        def _():
            each(lax.div(7 * (step - 5) + 1, 2), lax.div(7 * (step - 4) + 1, 2), tile)

    each(1, HALF + 1, ring_step)
    for t in (11, 12, 13):
        tile(t)
    sib_wait(2, 1)
    for r in range((rows_src + rows_tgt) // TILE):
        last_tile(r)

    lane = lax.broadcasted_iota(jnp.int32, (128, 128), 1)
    lane8 = lax.broadcasted_iota(jnp.int32, (8, 128), 1)
    sub8 = lax.broadcasted_iota(jnp.int32, (8, 128), 0)
    sub16 = lax.broadcasted_iota(jnp.int32, (16, 128), 0)
    used_rows = 2 * blocks_src + blocks_tgt
    is_cross = sub16 < blocks_src
    row_log = jnp.where((sub16 >= blocks_src) & (sub16 < 2 * blocks_src), log_src, log_tgt)

    def over_rows(count, body, init):
        for r in range(0, count, STEP):
            init = body(r, init)
        return init

    def zeros8(count):
        return tuple(jnp.zeros((8, 128), jnp.float32) for _ in range(count))

    def roll_flat(block, lanes, rows_on):
        rolled = pltpu.roll(block, lanes, 1)
        rolled = jnp.where(lane8 < lanes, pltpu.roll(rolled, 1, 0), rolled)
        return pltpu.roll(rolled, rows_on, 0)

    def turned(earlier, both, chips):
        flat = 2 * a * chips
        earlier = roll_flat(earlier, lax.rem(flat, 128), lax.div(flat, 128))
        flat = 2 * b * chips
        lanes, rows_on = lax.rem(flat, 128), lax.div(flat, 128)
        swapped = pltpu.roll(both, 4, 0)
        cross = roll_flat(jnp.where(sub8 < 4, both, swapped), lanes, rows_on)
        later = roll_flat(jnp.where(sub8 < 4, swapped, both), lanes, rows_on)
        return earlier, jnp.where(sub8 < 4, cross, later)

    chips_on = lax.rem(z + HALF + 1, NZ)

    def merged(parts, logs):
        total = tree(add, parts)
        if logs is None:
            return total
        top = tree(jnp.maximum, parts)
        return jnp.where((sub8 < 4) & logs, top + jnp.log2(tree(add, [jnp.exp2(p - top) for p in parts])), total)

    def lanes_at(h, first=0):
        return slice(first + 128 * h, first + 128 * h + 128)

    col_pot[0] = jnp.ones((8, 128), jnp.float32)
    col_pot[1] = jnp.where(sub8 < 4, 0.0, 1.0)

    def iteration(index):
        def src_rows_part(r):
            at = pl.ds(r, 32)
            values = [scores[at, lanes_at(h, cols_src)] + col_pot[1, h : h + 1] for h in range(lanes_tgt)]
            top = tree(jnp.maximum, values)
            best[at, :] = top
            acc_cross[at, :] = tree(add, [jnp.exp2(v - top) for v in values])
            acc[at, :] = tree(add, [scores[at, lanes_at(h)] * col_pot[0, h : h + 1] for h in range(lanes_src)])

        def tgt_rows_part(r):
            at = pl.ds(rows_src + r, 32)
            acc[at, :] = tree(
                add,
                [scores[at, lanes_at(h, cols_src)] * col_pot[1, 4 + h : 5 + h] for h in range(lanes_tgt)],
            )

        def in_parts(part):
            def body(r, carry):
                for k in range(STEP // 32):
                    part(r + 32 * k)
                return carry

            return body

        over_rows(rows_src, in_parts(src_rows_part), 0)
        over_rows(rows_tgt, in_parts(tgt_rows_part), 0)
        def over_sublanes(block, op, reduce):
            return reduce(fold_rows(block, op), axis=0, keepdims=True)

        for r in range(blocks_src + blocks_tgt):
            at = slice(128 * r, 128 * r + 128)
            if r < blocks_src:
                each_top = best[at, :].T
                top = over_sublanes(each_top, jnp.maximum, jnp.max)
                total = over_sublanes(acc_cross[at, :].T * jnp.exp2(each_top - top), add, jnp.sum)
                row_send[index, r : r + 1] = top + jnp.log2(total)
            row = blocks_src + r
            row_send[index, row : row + 1] = over_sublanes(acc[at, :].T, add, jnp.sum)
        row_recv[index, place] = row_send[index]
        sent = row_send.at[index, pl.ds(0, used_rows)]
        for k in range(1, PLANE):
            remote(
                sent,
                row_recv.at[index, place, pl.ds(0, used_rows)],
                row_ss.at[index],
                row_rs.at[index],
                plane_peer(k),
            ).start()
        others = row_recv.at[index, pl.ds(0, PLANE - 1), pl.ds(0, used_rows)]
        arrived(row_rs.at[index], others)
        parts = [row_recv[index, q] for q in range(PLANE)]
        top = tree(jnp.maximum, parts)
        spread = top + jnp.log2(tree(add, [jnp.exp2(p - top) for p in parts]))
        phi = row_log - jnp.where(is_cross, spread, jnp.log2(tree(add, parts)))
        phi_ref[...] = phi
        table = jnp.where(is_cross, phi, jnp.exp2(phi))
        table = jnp.concatenate([table, jnp.zeros((112, 128), jnp.float32)], axis=0).T
        for r in range(used_rows):
            pot[128 * r : 128 * r + 128, :] = jnp.broadcast_to(table[:, r : r + 1], (128, 128))

        def weighted_cols(first_row, first_col, first_pot, count, lanes):
            def body(r, sums):
                w = pot[pl.ds(first_pot + r, STEP), :]
                return tuple(
                    sums[h] + fold_rows(scores[pl.ds(first_row + r, STEP), lanes_at(h, first_col)] * w, add)
                    for h in range(lanes)
                )

            sums = over_rows(count, body, zeros8(lanes))
            return [jnp.sum(s, axis=0, keepdims=True) for s in sums]

        def cross_body(r, carry):
            w = pot[pl.ds(r, STEP), :]
            out = []
            for h in range(lanes_tgt):
                values = scores[pl.ds(r, STEP), lanes_at(h, cols_src)] + w
                top, total = carry[2 * h], carry[2 * h + 1]
                new_top = jnp.maximum(top, fold_rows(values, jnp.maximum))
                parts = [jnp.exp2(values[8 * k : 8 * k + 8] - new_top) for k in range(STEP // 8)]
                out += [new_top, total * jnp.exp2(top - new_top) + tree(add, parts)]
            return tuple(out)

        start = (jnp.full((8, 128), -1e30, jnp.float32), jnp.zeros((8, 128), jnp.float32))
        sums = over_rows(rows_src, cross_body, start * lanes_tgt)
        tops = [jnp.max(t, axis=0, keepdims=True) for t in sums[::2]]
        sums = [t * jnp.exp2(m - top) for t, m, top in zip(sums[1::2], sums[::2], tops)]
        both = [tops[h] + jnp.log2(jnp.sum(sums[h], axis=0, keepdims=True)) for h in range(lanes_tgt)]
        both = both + weighted_cols(rows_src, cols_src, 2 * rows_src, rows_tgt, lanes_tgt)
        earlier = weighted_cols(0, 0, rows_src, rows_src, lanes_src)
        blocks = turned(jnp.concatenate(earlier, axis=0), jnp.concatenate(both, axis=0), chips_on)
        weight = jnp.where(
            is_cross,
            1.0 / (n_src * SCALE),
            jnp.where(
                sub16 < 2 * blocks_src,
                -0.5 / (n_src * SCALE),
                jnp.where(sub16 < used_rows, -0.5 / (n_tgt * SCALE), 0.0),
            ),
        )
        extra = jnp.sum(phi * weight, axis=0, keepdims=True)

        size = 9
        me_near = 2 * z_near + core
        for k in range(2):
            near_send[index, k, 0:8] = blocks[k]
            near_send[index, k, 8:9] = jnp.zeros_like(extra) if k else extra
        near_recv[index, me_near] = near_send[index, core]

        def near_send_to(o):
            zn, cc = lax.rem(z_near + o // 2, NEAR), lax.rem(core + o % 2, 2)
            remote(
                near_send.at[index, cc, pl.ds(0, size)],
                near_recv.at[index, me_near, pl.ds(0, size)],
                near_ss.at[index],
                near_rs.at[index],
                device(x, y, NEAR * z_far + zn, cc),
            ).start()

        for o in range(1, 2 * NEAR):
            near_send_to(o)
        others = near_recv.at[index, pl.ds(0, 2 * NEAR - 1), pl.ds(0, size)]
        arrived(near_rs.at[index], others)
        me_far = 2 * z_far + core
        block = merged([near_recv[index, q, 0:8] for q in range(2 * NEAR)], core == 1)
        extra = tree(add, [near_recv[index, q, 8:9] for q in range(2 * NEAR)])
        far_send[index, 0:8] = block
        far_send[index, 8:9] = extra
        far_recv[index, me_far, 0:8] = block
        far_recv[index, me_far, 8:9] = extra

        def far_send_to(o):
            zf, cc = lax.rem(z_far + o // 2, FAR), lax.rem(core + o % 2, 2)
            remote(
                far_send.at[index, pl.ds(0, size)],
                far_recv.at[index, me_far, pl.ds(0, size)],
                far_ss.at[index],
                far_rs.at[index],
                device(x, y, NEAR * zf + z_near, cc),
            ).start()

        for o in range(1, 2 * FAR):
            far_send_to(o)
        others = far_recv.at[index, pl.ds(0, 2 * FAR - 1), pl.ds(0, size)]
        arrived(far_rs.at[index], others)
        earlier = merged([far_recv[index, 2 * q, 0:8] for q in range(FAR)], None)
        both = merged([far_recv[index, 2 * q + 1, 0:8] for q in range(FAR)], True)
        totals[0] = earlier
        totals[1] = both
        totals[2, 0:1] = tree(add, [far_recv[index, 2 * q, 8:9] for q in range(FAR)])

        @pl.when(index == 0)
        def _():
            earlier_pot, both_pot = turned(
                n_src / earlier,
                jnp.where(sub8 < 4, log_src - both, n_tgt / both),
                lax.rem(NZ - chips_on, NZ),
            )
            col_pot[0] = earlier_pot
            col_pot[1] = both_pot

    each(0, ITERS, iteration)

    earlier, both = totals[0], totals[1]
    both = (1.0 / SCALE) * jnp.where(sub8 < 4, log_src - both, log_tgt - jnp.log2(both))
    earlier = (1.0 / SCALE) * (log_src - jnp.log2(earlier))
    share = jnp.where(sub8 < 4, 1.0 / n_tgt, -0.5 / n_tgt) * both - (0.5 / n_src) * earlier
    share = jnp.sum(share, axis=0, keepdims=True)

    sum_send[...] = share
    sum_recv[place] = share
    for k in range(1, PLANE):
        remote(sum_send, sum_recv.at[place], sum_ss.at[0], sum_rs.at[0], plane_peer(k)).start()

    def front(block, at, size):
        per = 128 // size
        return pltpu.roll(
            pltpu.roll(block, lax.rem(8 - lax.div(at, per), 8), 0),
            lax.rem(128 - size * lax.rem(at, per), 128),
            1,
        )

    duals = phi_ref[...] * (1.0 / SCALE)
    src_rows = front(duals[0:8], place, a)
    tgt_rows = front(duals[8:16], place, b)
    tgt_cols = front(both, 2 * z + core, b)
    returned = jnp.where(
        sub8 == 1,
        pltpu.roll(src_rows, 5, 0),
        jnp.where(
            sub8 == 2,
            pltpu.roll(tgt_rows, 2, 0),
            jnp.where(sub8 == 3, pltpu.roll(tgt_cols, 3, 0), src_rows),
        ),
    )
    gone(gather_ss.at[0], cols.at[pl.ds(0, UNIT * (2 * HALF - 1) * UNITS), pl.ds(0, width)])
    gone(gather_ss.at[1], cols.at[pl.ds(0, NZ * (a + b))])
    gone(gather_ss.at[2], rows.at[pl.ds(0, UNIT * (PLANE - 1) * UNITS)])
    for index in range(ITERS):
        gone(row_ss.at[index], row_recv.at[index, pl.ds(0, PLANE - 1), pl.ds(0, used_rows)])
        gone(near_ss.at[index], near_recv.at[index, pl.ds(0, 2 * NEAR - 1), pl.ds(0, 9)])
        gone(far_ss.at[index], far_recv.at[index, pl.ds(0, 2 * FAR - 1), pl.ds(0, 9)])
    others = sum_recv.at[pl.ds(0, PLANE - 1)]
    arrived(sum_rs.at[0], others)
    share = totals[2, 0:1] + tree(add, [sum_recv[q] for q in range(PLANE)])
    out_ref[...] = jnp.where(sub8 == 4, jnp.sum(share, axis=1, keepdims=True), returned)
    gone(sum_ss.at[0], others)


def hand_out(block_ref, left_ref, right_ref, earlier_ref, later_ref, div_ref):
    for k, ref in enumerate((left_ref, earlier_ref, later_ref, right_ref, div_ref)):
        ref[...] = block_ref[k : k + 1, 0 : ref.shape[1]]


def per_device(earlier_vectors, later_vectors):
    a, width = earlier_vectors.shape
    b = later_vectors.shape[0]
    rows_src, rows_tgt = a * PLANE, b * PLANE
    cols_src, cols_tgt = 2 * a * NZ, 2 * b * NZ
    rows_all, cols_all = rows_src + rows_tgt, cols_src + cols_tgt
    f32, bf16 = jnp.float32, jnp.bfloat16
    dma = pltpu.SemaphoreType.DMA
    wide = width + 128
    block = pl.pallas_call(
        kernel,
        out_shape=jax.ShapeDtypeStruct((8, 128), f32),
        in_specs=[pl.BlockSpec(memory_space=pltpu.HBM)] * 2,
        out_specs=pl.BlockSpec(memory_space=pltpu.VMEM),
        scratch_shapes=[
            pltpu.VMEM((rows_all, wide), bf16),
            pltpu.VMEM((cols_all + 128, wide), bf16),
            pltpu.VMEM((rows_all, cols_all), f32),
            pltpu.VMEM((rows_src, 128), f32),
            pltpu.VMEM((rows_all, 128), f32),
            pltpu.VMEM((rows_src, 128), f32),
            pltpu.VMEM((2 * rows_src + rows_tgt, 128), f32),
            pltpu.VMEM((2, 8, 128), f32),
            pltpu.VMEM((16, 128), f32),
            pltpu.VMEM((3, 8, 128), f32),
            pltpu.VMEM((ITERS, 16, 128), f32),
            pltpu.VMEM((ITERS, PLANE, 16, 128), f32),
            pltpu.VMEM((ITERS, 2, 16, 128), f32),
            pltpu.VMEM((ITERS, 2 * NEAR, 16, 128), f32),
            pltpu.VMEM((ITERS, 16, 128), f32),
            pltpu.VMEM((ITERS, 2 * FAR, 16, 128), f32),
            pltpu.VMEM((1, 128), f32),
            pltpu.VMEM((PLANE, 1, 128), f32),
            dma((4,)),
            dma((2 * HALF * UNITS,)),
            dma((3,)),
            dma((4 * UNITS,)),
            dma((16 * UNITS,)),
            dma((1,)),
            dma((3,)),
            dma((ITERS,)),
            dma((ITERS,)),
            dma((ITERS,)),
            dma((ITERS,)),
            dma((ITERS,)),
            dma((ITERS,)),
            dma((1,)),
            dma((1,)),
        ],
        compiler_params=pltpu.CompilerParams(
            collective_id=0, has_side_effects=True, vmem_limit_bytes=60 * 1024 * 1024
        ),
        cost_estimate=pl.CostEstimate(
            flops=2 * wide * (rows_src * cols_all + rows_tgt * cols_tgt),
            bytes_accessed=2 * width * (a + b),
            transcendentals=rows_src * (cols_src + 3 * cols_tgt) + rows_tgt * cols_tgt,
        ),
    )(earlier_vectors, later_vectors)
    vmem = pl.BlockSpec(memory_space=pltpu.VMEM)
    left, right, earlier, later, div = pl.pallas_call(
        hand_out,
        out_shape=tuple(jax.ShapeDtypeStruct(s, f32) for s in ((1, a), (1, b), (1, a), (1, b), (1, 1))),
        in_specs=[vmem],
        out_specs=(vmem,) * 5,
    )(block)
    return left.reshape(a), right.reshape(b), earlier.reshape(a), later.reshape(b), div.reshape(())


def solution(mesh):
    return jax.shard_map(
        per_device,
        mesh=mesh,
        in_specs=(P(("row", "col"), None), P(("row", "col"), None)),
        out_specs=(P(("row", "col")), P(("row", "col")), P(("row", "col")), P(("row", "col")), P()),
        check_vma=False,
    )
```

```python
import functools

import jax
import jax.numpy as jnp
import numpy as np
from jax import lax
from jax.experimental import pallas as pl
from jax.experimental.pallas import tpu as pltpu
from jax.sharding import PartitionSpec as P

EPSILON = 0.04
ITERS = 2
MESH = pl.DeviceIdType.MESH

NX, NY, NZ = 4, 4, 16
PLANE = NX * NY
HALF = NZ // 2
NEAR = 4
FAR = NZ // NEAR
UNIT = 16
UNITS = 3
TILE = 256
STEP = 128
SCALE = float(np.log2(np.e)) / EPSILON


def add(a, b):
    return a + b


def tree(op, parts):
    while len(parts) > 1:
        parts = [op(parts[i], parts[i + 1]) for i in range(0, len(parts) - 1, 2)] + (
            [parts[-1]] if len(parts) % 2 else []
        )
    return parts[0]


def fold_rows(x, op):
    return tree(op, [x[8 * k : 8 * k + 8] for k in range(x.shape[0] // 8)])


def quotient(number, by):
    return number // by if isinstance(number, int) else lax.div(number, by)


def multiple(number, of):
    return number if isinstance(number, int) else pl.multiple_of(number, of)


def each(lower, upper, body):
    def step(k, carry):
        body(k)
        return carry

    lax.fori_loop(lower, upper, step, 0)


def kernel(
    src_ref,
    tgt_ref,
    out_ref,
    rows,
    cols,
    scores,
    best,
    acc,
    acc_cross,
    pot,
    col_pot,
    phi_ref,
    totals,
    row_send,
    row_recv,
    near_send,
    near_recv,
    far_send,
    far_recv,
    sum_send,
    sum_recv,
    own_sem,
    z_rs,
    sib_rs,
    first_rs,
    second_rs,
    onward_rs,
    gather_ss,
    row_ss,
    row_rs,
    near_ss,
    near_rs,
    far_ss,
    far_rs,
    sum_ss,
    sum_rs,
):
    a, width = src_ref.shape
    b = tgt_ref.shape[0]
    n_src, n_tgt = a * PLANE * NZ * 2, b * PLANE * NZ * 2
    log_src, log_tgt = float(np.log2(n_src)), float(np.log2(n_tgt))
    rows_src, rows_tgt = a * PLANE, b * PLANE
    cols_src, cols_tgt = a * NZ * 2, b * NZ * 2
    last = cols_src + cols_tgt
    lanes_src, lanes_tgt = cols_src // 128, cols_tgt // 128
    blocks_src, blocks_tgt = rows_src // 128, rows_tgt // 128

    row, col = lax.axis_index("row"), lax.axis_index("col")
    y, z = lax.div(row, NZ), lax.rem(row, NZ)
    x, core = lax.div(col, 2), lax.rem(col, 2)
    other = 1 - core
    place = y * NX + x

    def device(xx, yy, zz, cc):
        return (yy * NZ + zz, xx * 2 + cc)

    def remote(src, dst, ss, rs, to):
        return pltpu.make_async_remote_copy(
            src_ref=src, dst_ref=dst, send_sem=ss, recv_sem=rs, device_id=to, device_id_type=MESH
        )

    def plane_peer(k):
        q = lax.rem(place + k, PLANE)
        return device(lax.rem(q, NX), lax.div(q, NX), z, core)

    z_near, z_far = lax.rem(z, NEAR), lax.div(z, NEAR)
    up, down = device(x, y, lax.rem(z + 1, NZ), core), device(x, y, lax.rem(z + NZ - 1, NZ), core)

    def arrived(sem, at):
        remote(at, at, sem, sem, up).wait_recv()

    def gone(sem, at):
        remote(at, at, sem, sem, up).wait_send()

    barrier = pltpu.get_barrier_semaphore()
    greeted = [
        up,
        down,
        device(x, y, z, other),
        device(lax.rem(x + 1, NX), y, z, core),
        device(lax.rem(x + NX - 1, NX), y, z, core),
        device(x, lax.rem(y + 1, NY), z, core),
        device(x, lax.rem(y + NY - 1, NY), z, core),
    ]
    for to in greeted:
        pl.semaphore_signal(barrier, inc=1, device_id=to, device_id_type=MESH)

    MIDDLE = HALF - 1

    def src_start(pos, at_last, c):
        usual = 2 * a * pos
        return pl.multiple_of(usual + at_last * (last + 2 * a - usual) + a * c, UNIT)

    def tgt_start(pos, at_last, c):
        quarter = lax.div(pos + NZ // 4, NZ // 2)
        stored = pos + quarter * (12 - 8 * quarter) * (NZ // 16)
        usual = cols_src + 2 * b * stored
        return pl.multiple_of(usual + at_last * (last - usual) + b * c, UNIT)

    def unit_start(pos, at_last, u):
        if u == 2:
            return tgt_start(pos, at_last, core)
        return pl.multiple_of(src_start(pos, at_last, core) + UNIT * u, UNIT)

    def z_copy(flow, step, u):
        way = 1 - 2 * flow
        at = (flow * HALF + step - 1) * UNITS + u
        before = unit_start(MIDDLE + way * (step - 1), 0, u)
        after = unit_start(MIDDLE + way * step, lax.div(step, HALF), u)
        return remote(
            cols.at[pl.ds(before, UNIT), pl.ds(0, width)],
            cols.at[pl.ds(after, UNIT), pl.ds(0, width)],
            gather_ss.at[0],
            z_rs.at[at],
            up if flow else down,
        )

    def sib_send(step, pos):
        at_last = lax.div(step, HALF)
        sem = lax.div(step + 3, HALF) + at_last
        for start, size in ((src_start(pos, at_last, core), a), (tgt_start(pos, at_last, core), b)):
            at = cols.at[pl.ds(start, size)]
            remote(at, at, gather_ss.at[1], sib_rs.at[sem], device(x, y, z, other)).start()

    def sib_wait(sem, slots):
        arrived(sib_rs.at[sem], cols.at[pl.ds(0, slots * (a + b))])

    def shifted(u, first, second):
        later = lax.div(u * (u - 1), 2)
        f = lax.div((1 - u) * (2 - u), 2) + later * (1 - core)
        xx = lax.rem(x + f * first + (1 - f) * second, NX)
        yy = lax.rem(y + f * second + (1 - f) * first, NY)
        q = yy * NX + xx
        start = (a - (a - b) * later) * q + UNIT * u * (1 - later) + rows_src * later
        return device(xx, yy, z, core), rows.at[pl.ds(pl.multiple_of(start, UNIT), UNIT)]

    def plane_copy(at, sem, to):
        return remote(at, at, gather_ss.at[2], sem, to)

    def first_send(u, k):
        plane_copy(shifted(u, 0, 0)[1], first_rs.at[4 * u + k], shifted(u, k, 0)[0]).start()

    def first_arrival(u, k):
        arrived(first_rs.at[4 * u + k], shifted(u, 4 - k, 0)[1])

    def first_onward(u):
        way = 1 + 2 * lax.rem(u, 2)
        plane_copy(shifted(u, 4 - way, 0)[1], first_rs.at[4 * u + 2], shifted(u, way, 0)[0]).start()

    def second_sends(u, j):
        for k in (1, 3):
            sem = second_rs.at[4 * (4 * u + j) + k]
            plane_copy(shifted(u, 4 - j, 0)[1], sem, shifted(u, 0, k)[0]).start()

    def second_onward(u, j):
        for k in (1, 3):
            arrived(second_rs.at[4 * (4 * u + j) + k], shifted(u, 4 - j, 4 - k)[1])
        way = 1 + 2 * lax.rem(j, 2)
        plane_copy(shifted(u, 4 - j, 4 - way)[1], onward_rs.at[0], shifted(u, 0, way)[0]).start()

    def norm_lanes(source, start, size, targets):
        lane_own = lax.broadcasted_iota(jnp.int32, (size, 128), 1)
        v = source[pl.ds(start, size), 0:width].astype(jnp.float32)
        v = v * v
        total = tree(add, [v[:, 128 * h : 128 * h + 128] for h in range(width // 128)])
        rest = -0.5 * jnp.sum(total, axis=1, keepdims=True)
        terms = []
        for _ in range(3):
            term = rest.astype(jnp.bfloat16).astype(jnp.float32)
            rest = rest - term
            terms.append(term)
        for target, at, first in targets:
            more = jnp.where(lane_own < 6, 1.0, 0.0)
            for k, term in enumerate(terms):
                more = jnp.where(lane_own == first + k, term, more)
            target[pl.ds(at, size), width : width + 128] = more.astype(jnp.bfloat16)

    mine = (
        (src_ref, a, pl.multiple_of(a * place, UNIT), src_start(MIDDLE, 0, core)),
        (tgt_ref, b, pl.multiple_of(rows_src + b * place, UNIT), tgt_start(MIDDLE, 0, core)),
    )
    own_copies = []
    for kind, (ref, size, as_row, as_col) in enumerate(mine):
        for k, (target, at) in enumerate(((rows, as_row), (cols, as_col))):
            own_copies.append(
                pltpu.make_async_copy(
                    ref, target.at[pl.ds(at, size), pl.ds(0, width)], own_sem.at[2 * kind + k]
                )
            )
    for copy in own_copies:
        copy.start()
    row_recv[...] = jnp.ones(row_recv.shape, jnp.float32)
    row_send[...] = jnp.ones(row_send.shape, jnp.float32)
    for copy in own_copies:
        copy.wait()
    pl.semaphore_wait(barrier, len(greeted))

    for u in range(UNITS):
        z_copy(0, 1, u).start()
        z_copy(1, 1, u).start()
    for _, size, as_row, as_col in mine:
        norm_lanes(rows, as_row, size, [(rows, as_row, 0), (cols, as_col, 3)])

    def plane_start(u):
        first_send(u, 1)
        first_send(u, 3)

    each(0, UNITS, plane_start)
    each(0, UNITS, lambda u: second_sends(u, 0))
    sib_send(0, MIDDLE)

    outer_end = cols_src + cols_tgt // 2
    empty = jnp.zeros((2 * a, width + 128), jnp.bfloat16)
    cols[cols_src - 2 * a : cols_src, :] = empty
    cols[outer_end - 2 * b : outer_end, :] = empty[: 2 * b]
    cols[last + 2 * b : last + 2 * a, :] = empty[: 2 * a - 2 * b]

    def product(r, start, size):
        at = pl.ds(multiple(r * TILE, TILE), TILE)
        cross = lax.dot_general(
            rows[at, :],
            cols[pl.ds(multiple(start, 128), size), :],
            (((1,), (1,)), ((), ())),
            preferred_element_type=jnp.float32,
        )
        return at, [cross[:, 128 * h : 128 * h + 128] * SCALE for h in range(size // 128)]

    def tile(t):
        outer, i = quotient(t, 7), t - 7 * quotient(t, 7)
        is_tgt, pair = quotient(i, 4), quotient(i, 2)
        r = i - 2 * pair + 2 * quotient(i, 6)
        g = (1 - outer) * (1 + pair) + outer * 3 * pair
        at, (one, two) = product(
            r, (1 - is_tgt) * TILE * g + is_tgt * (cols_src + (1 - outer) * (cols_tgt // 2)), TILE
        )
        is_self = (i < 4) | (i == 6)
        lane_one = (1 - is_tgt) * TILE * g + is_tgt * (cols_src + 128 * (1 - outer))
        lane_two = (1 - is_tgt) * (TILE * g + 128) + is_tgt * (cols_src + 256 + 128 * outer)
        for value, lanes in ((one, lane_one), (two, lane_two)):
            if isinstance(t, int):
                value = jnp.exp2(value) if is_self else value
            else:
                value = jnp.where(is_self, jnp.exp2(value), value)
            scores[at, pl.ds(multiple(lanes, 128), 128)] = value

    lane1 = lax.broadcasted_iota(jnp.int32, (1, 128), 1)

    def last_tile(r):
        at, (value,) = product(r, last, 128)
        e = jnp.exp2(value)
        src_lanes, tgt_lanes = slice(cols_src - 128, cols_src), slice(last - 128, last)
        scores[at, src_lanes] = jnp.where(lane1 >= 2 * a, e, scores[at, src_lanes])
        moved = pltpu.roll(value if r * TILE < rows_src else e, 128 - 2 * b, 1)
        scores[at, tgt_lanes] = jnp.where(lane1 >= 128 - 2 * b, moved, scores[at, tgt_lanes])

    def ring_step(step):
        for u in range(UNITS):
            for flow in range(2):
                longer = 1 if flow == (1 if u == 1 else 0) else 0
                steps = HALF - 1 + longer + core * (1 - 2 * longer)

                @pl.when(step <= steps)
                def _():
                    z_copy(flow, step, u).wait_recv()

                @pl.when(step < steps)
                def _():
                    z_copy(flow, step + 1, u).start()

        def to_other(flow):
            pos = MIDDLE + (1 - 2 * flow) * step
            at_last = lax.div(step, HALF)
            for start, size in ((src_start(pos, at_last, core), a), (tgt_start(pos, at_last, core), b)):
                norm_lanes(cols, start, size, [(cols, start, 3)])
            sib_send(step, pos)

        each(0, 2 - lax.div(step, HALF), to_other)

        @pl.when(step == 1)
        def _():
            def stage(u):
                first_arrival(u, 1)
                first_arrival(u, 3)
                first_onward(u)
                second_sends(u, 1)
                second_sends(u, 3)

            each(0, UNITS, stage)

        @pl.when(step == 2)
        def _():
            def stage(u):
                first_arrival(u, 2)
                second_sends(u, 2)

            each(0, UNITS, stage)

        @pl.when((step >= 2) & (step <= 4))
        def _():
            def stage(i):
                u, k = lax.rem(i, UNITS), lax.div(i, UNITS)
                second_onward(u, k + lax.div(k, 2) - 2 * lax.div(k, 3))

            each(
                UNITS * (2 * step - 4 - lax.div(step, 3)),
                UNITS * (2 * step - 3 - lax.div(step, 4)),
                stage,
            )

        @pl.when(step == 5)
        def _():
            arrived(onward_rs.at[0], rows.at[pl.ds(0, 4 * UNITS * UNIT)])
            sib_wait(0, 9)

        @pl.when(step == 7)
        def _():
            sib_wait(1, 6)

        @pl.when((step >= 5) & (step < HALF))
        def _():
            each(lax.div(7 * (step - 5) + 1, 2), lax.div(7 * (step - 4) + 1, 2), tile)

    each(1, HALF + 1, ring_step)
    for t in (11, 12, 13):
        tile(t)
    sib_wait(2, 1)
    for r in range((rows_src + rows_tgt) // TILE):
        last_tile(r)

    lane = lax.broadcasted_iota(jnp.int32, (128, 128), 1)
    lane8 = lax.broadcasted_iota(jnp.int32, (8, 128), 1)
    sub8 = lax.broadcasted_iota(jnp.int32, (8, 128), 0)
    sub16 = lax.broadcasted_iota(jnp.int32, (16, 128), 0)
    used_rows = 2 * blocks_src + blocks_tgt
    is_cross = sub16 < blocks_src
    row_log = jnp.where((sub16 >= blocks_src) & (sub16 < 2 * blocks_src), log_src, log_tgt)

    def over_rows(count, body, init):
        for r in range(0, count, STEP):
            init = body(r, init)
        return init

    def zeros8(count):
        return tuple(jnp.zeros((8, 128), jnp.float32) for _ in range(count))

    def roll_flat(block, lanes, rows_on):
        rolled = pltpu.roll(block, lanes, 1)
        rolled = jnp.where(lane8 < lanes, pltpu.roll(rolled, 1, 0), rolled)
        return pltpu.roll(rolled, rows_on, 0)

    def turned(earlier, both, chips):
        flat = 2 * a * chips
        earlier = roll_flat(earlier, lax.rem(flat, 128), lax.div(flat, 128))
        flat = 2 * b * chips
        lanes, rows_on = lax.rem(flat, 128), lax.div(flat, 128)
        swapped = pltpu.roll(both, 4, 0)
        cross = roll_flat(jnp.where(sub8 < 4, both, swapped), lanes, rows_on)
        later = roll_flat(jnp.where(sub8 < 4, swapped, both), lanes, rows_on)
        return earlier, jnp.where(sub8 < 4, cross, later)

    chips_on = lax.rem(z + HALF + 1, NZ)

    def merged(parts, logs):
        total = tree(add, parts)
        if logs is None:
            return total
        top = tree(jnp.maximum, parts)
        return jnp.where((sub8 < 4) & logs, top + jnp.log2(tree(add, [jnp.exp2(p - top) for p in parts])), total)

    def lanes_at(h, first=0):
        return slice(first + 128 * h, first + 128 * h + 128)

    def iteration(index):
        def src_rows_part(r):
            at = pl.ds(r, 32)
            values = [scores[at, lanes_at(h, cols_src)] for h in range(lanes_tgt)]
            if index == 0:
                top = tree(jnp.maximum, values)
                best[at, :] = top
                acc_cross[at, :] = tree(add, [jnp.exp2(v - top) for v in values])
                acc[at, :] = tree(add, [scores[at, lanes_at(h)] for h in range(lanes_src)])
                return
            w = pot[at, :]
            values = [jnp.exp2(v + w + col_pot[1, h : h + 1]) for h, v in enumerate(values)]
            for h, v in enumerate(values):
                scores[at, lanes_at(h, cols_src)] = v
            acc_cross[at, :] = tree(add, values)
            acc[at, :] = tree(add, [scores[at, lanes_at(h)] * col_pot[0, h : h + 1] for h in range(lanes_src)])

        def tgt_rows_part(r):
            at = pl.ds(rows_src + r, 32)
            acc[at, :] = tree(
                add,
                [
                    scores[at, lanes_at(h, cols_src)] * (col_pot[1, 4 + h : 5 + h] if index else 1.0)
                    for h in range(lanes_tgt)
                ],
            )

        def in_parts(part):
            def body(r, carry):
                for k in range(STEP // 32):
                    part(r + 32 * k)
                return carry

            return body

        over_rows(rows_src, in_parts(src_rows_part), 0)
        over_rows(rows_tgt, in_parts(tgt_rows_part), 0)
        def over_sublanes(block, op, reduce):
            return reduce(fold_rows(block, op), axis=0, keepdims=True)

        for r in range(blocks_src + blocks_tgt):
            at = slice(128 * r, 128 * r + 128)
            if r < blocks_src and index:
                row_send[index, r : r + 1] = over_sublanes(acc_cross[at, :].T, add, jnp.sum)
            elif r < blocks_src:
                each_top = best[at, :].T
                top = over_sublanes(each_top, jnp.maximum, jnp.max)
                total = over_sublanes(acc_cross[at, :].T * jnp.exp2(each_top - top), add, jnp.sum)
                row_send[index, r : r + 1] = top + jnp.log2(total)
            row = blocks_src + r
            row_send[index, row : row + 1] = over_sublanes(acc[at, :].T, add, jnp.sum)
        row_recv[index, place] = row_send[index]
        sent = row_send.at[index, pl.ds(0, used_rows)]
        for k in range(1, PLANE):
            remote(
                sent,
                row_recv.at[index, place, pl.ds(0, used_rows)],
                row_ss.at[index],
                row_rs.at[index],
                plane_peer(k),
            ).start()
        others = row_recv.at[index, pl.ds(0, PLANE - 1), pl.ds(0, used_rows)]
        arrived(row_rs.at[index], others)
        parts = [row_recv[index, q] for q in range(PLANE)]
        change = row_log - jnp.log2(tree(add, parts))
        if index == 0:
            top = tree(jnp.maximum, parts)
            spread = top + jnp.log2(tree(add, [jnp.exp2(p - top) for p in parts]))
            phi = jnp.where(is_cross, row_log - spread, change)
            table = jnp.where(is_cross, phi, jnp.exp2(phi))
        else:
            phi = jnp.where(is_cross, phi_ref[...] + change, change)
            table = jnp.exp2(change)
        phi_ref[...] = phi
        table = jnp.concatenate([table, jnp.zeros((112, 128), jnp.float32)], axis=0).T
        for r in range(used_rows):
            pot[128 * r : 128 * r + 128, :] = jnp.broadcast_to(table[:, r : r + 1], (128, 128))

        def weighted_cols(first_row, first_col, first_pot, count, lanes):
            def body(r, sums):
                w = pot[pl.ds(first_pot + r, STEP), :]
                return tuple(
                    sums[h] + fold_rows(scores[pl.ds(first_row + r, STEP), lanes_at(h, first_col)] * w, add)
                    for h in range(lanes)
                )

            sums = over_rows(count, body, zeros8(lanes))
            return [jnp.sum(s, axis=0, keepdims=True) for s in sums]

        def cross_body(r, carry):
            w = pot[pl.ds(r, STEP), :]
            out = []
            for h in range(lanes_tgt):
                values = scores[pl.ds(r, STEP), lanes_at(h, cols_src)] + w
                top, total = carry[2 * h], carry[2 * h + 1]
                new_top = jnp.maximum(top, fold_rows(values, jnp.maximum))
                parts = [jnp.exp2(values[8 * k : 8 * k + 8] - new_top) for k in range(STEP // 8)]
                out += [new_top, total * jnp.exp2(top - new_top) + tree(add, parts)]
            return tuple(out)

        if index == 0:
            start = (jnp.full((8, 128), -1e30, jnp.float32), jnp.zeros((8, 128), jnp.float32))
            sums = over_rows(rows_src, cross_body, start * lanes_tgt)
            tops = [jnp.max(t, axis=0, keepdims=True) for t in sums[::2]]
            sums = [t * jnp.exp2(m - top) for t, m, top in zip(sums[1::2], sums[::2], tops)]
            both = [tops[h] + jnp.log2(jnp.sum(sums[h], axis=0, keepdims=True)) for h in range(lanes_tgt)]
        else:
            both = weighted_cols(0, cols_src, 0, rows_src, lanes_tgt)
        both = both + weighted_cols(rows_src, cols_src, 2 * rows_src, rows_tgt, lanes_tgt)
        earlier = weighted_cols(0, 0, rows_src, rows_src, lanes_src)
        blocks = turned(jnp.concatenate(earlier, axis=0), jnp.concatenate(both, axis=0), chips_on)
        weight = jnp.where(
            is_cross,
            1.0 / (n_src * SCALE),
            jnp.where(
                sub16 < 2 * blocks_src,
                -0.5 / (n_src * SCALE),
                jnp.where(sub16 < used_rows, -0.5 / (n_tgt * SCALE), 0.0),
            ),
        )
        extra = jnp.sum(phi * weight, axis=0, keepdims=True)

        size = 9
        me_near = 2 * z_near + core
        for k in range(2):
            near_send[index, k, 0:8] = blocks[k]
            near_send[index, k, 8:9] = jnp.zeros_like(extra) if k else extra
        near_recv[index, me_near] = near_send[index, core]

        def near_send_to(o):
            zn, cc = lax.rem(z_near + o // 2, NEAR), lax.rem(core + o % 2, 2)
            remote(
                near_send.at[index, cc, pl.ds(0, size)],
                near_recv.at[index, me_near, pl.ds(0, size)],
                near_ss.at[index],
                near_rs.at[index],
                device(x, y, NEAR * z_far + zn, cc),
            ).start()

        for o in range(1, 2 * NEAR):
            near_send_to(o)
        others = near_recv.at[index, pl.ds(0, 2 * NEAR - 1), pl.ds(0, size)]
        arrived(near_rs.at[index], others)
        me_far = 2 * z_far + core
        block = merged([near_recv[index, q, 0:8] for q in range(2 * NEAR)], None if index else core == 1)
        extra = tree(add, [near_recv[index, q, 8:9] for q in range(2 * NEAR)])
        far_send[index, 0:8] = block
        far_send[index, 8:9] = extra
        far_recv[index, me_far, 0:8] = block
        far_recv[index, me_far, 8:9] = extra

        def far_send_to(o):
            zf, cc = lax.rem(z_far + o // 2, FAR), lax.rem(core + o % 2, 2)
            remote(
                far_send.at[index, pl.ds(0, size)],
                far_recv.at[index, me_far, pl.ds(0, size)],
                far_ss.at[index],
                far_rs.at[index],
                device(x, y, NEAR * zf + z_near, cc),
            ).start()

        for o in range(1, 2 * FAR):
            far_send_to(o)
        others = far_recv.at[index, pl.ds(0, 2 * FAR - 1), pl.ds(0, size)]
        arrived(far_rs.at[index], others)
        earlier = merged([far_recv[index, 2 * q, 0:8] for q in range(FAR)], None)
        both = merged([far_recv[index, 2 * q + 1, 0:8] for q in range(FAR)], None if index else True)
        totals[0] = earlier
        totals[1] = both
        totals[2, 0:1] = tree(add, [far_recv[index, 2 * q, 8:9] for q in range(FAR)])

        if index == 0:
            gamma = log_src - both
            totals[3] = gamma
            earlier_pot, both_pot = turned(
                n_src / earlier, jnp.where(sub8 < 4, gamma, n_tgt / both), lax.rem(NZ - chips_on, NZ)
            )
            col_pot[0] = earlier_pot
            col_pot[1] = both_pot

    for index in range(ITERS):
        iteration(index)

    earlier, both = totals[0], totals[1]
    both = (1.0 / SCALE) * (jnp.where(sub8 < 4, totals[3] + log_src, log_tgt) - jnp.log2(both))
    earlier = (1.0 / SCALE) * (log_src - jnp.log2(earlier))
    share = jnp.where(sub8 < 4, 1.0 / n_tgt, -0.5 / n_tgt) * both - (0.5 / n_src) * earlier
    share = jnp.sum(share, axis=0, keepdims=True)

    sum_send[...] = share
    sum_recv[place] = share
    for k in range(1, PLANE):
        remote(sum_send, sum_recv.at[place], sum_ss.at[0], sum_rs.at[0], plane_peer(k)).start()

    def front(block, at, size):
        per = 128 // size
        return pltpu.roll(
            pltpu.roll(block, lax.rem(8 - lax.div(at, per), 8), 0),
            lax.rem(128 - size * lax.rem(at, per), 128),
            1,
        )

    duals = phi_ref[...] * (1.0 / SCALE)
    src_rows = front(duals[0:8], place, a)
    tgt_rows = front(duals[8:16], place, b)
    tgt_cols = front(both, 2 * z + core, b)
    returned = jnp.where(
        sub8 == 1,
        pltpu.roll(src_rows, 5, 0),
        jnp.where(
            sub8 == 2,
            pltpu.roll(tgt_rows, 2, 0),
            jnp.where(sub8 == 3, pltpu.roll(tgt_cols, 3, 0), src_rows),
        ),
    )
    gone(gather_ss.at[0], cols.at[pl.ds(0, UNIT * (2 * HALF - 1) * UNITS), pl.ds(0, width)])
    gone(gather_ss.at[1], cols.at[pl.ds(0, NZ * (a + b))])
    gone(gather_ss.at[2], rows.at[pl.ds(0, UNIT * (PLANE - 1) * UNITS)])
    for index in range(ITERS):
        gone(row_ss.at[index], row_recv.at[index, pl.ds(0, PLANE - 1), pl.ds(0, used_rows)])
        gone(near_ss.at[index], near_recv.at[index, pl.ds(0, 2 * NEAR - 1), pl.ds(0, 9)])
        gone(far_ss.at[index], far_recv.at[index, pl.ds(0, 2 * FAR - 1), pl.ds(0, 9)])
    others = sum_recv.at[pl.ds(0, PLANE - 1)]
    arrived(sum_rs.at[0], others)
    share = totals[2, 0:1] + tree(add, [sum_recv[q] for q in range(PLANE)])
    out_ref[...] = jnp.where(sub8 == 4, jnp.sum(share, axis=1, keepdims=True), returned)
    gone(sum_ss.at[0], others)


def hand_out(block_ref, left_ref, right_ref, earlier_ref, later_ref, div_ref):
    for k, ref in enumerate((left_ref, earlier_ref, later_ref, right_ref, div_ref)):
        ref[...] = block_ref[k : k + 1, 0 : ref.shape[1]]


def per_device(earlier_vectors, later_vectors):
    a, width = earlier_vectors.shape
    b = later_vectors.shape[0]
    rows_src, rows_tgt = a * PLANE, b * PLANE
    cols_src, cols_tgt = 2 * a * NZ, 2 * b * NZ
    rows_all, cols_all = rows_src + rows_tgt, cols_src + cols_tgt
    f32, bf16 = jnp.float32, jnp.bfloat16
    dma = pltpu.SemaphoreType.DMA
    wide = width + 128
    block = pl.pallas_call(
        kernel,
        out_shape=jax.ShapeDtypeStruct((8, 128), f32),
        in_specs=[pl.BlockSpec(memory_space=pltpu.HBM)] * 2,
        out_specs=pl.BlockSpec(memory_space=pltpu.VMEM),
        scratch_shapes=[
            pltpu.VMEM((rows_all, wide), bf16),
            pltpu.VMEM((cols_all + 128, wide), bf16),
            pltpu.VMEM((rows_all, cols_all), f32),
            pltpu.VMEM((rows_src, 128), f32),
            pltpu.VMEM((rows_all, 128), f32),
            pltpu.VMEM((rows_src, 128), f32),
            pltpu.VMEM((2 * rows_src + rows_tgt, 128), f32),
            pltpu.VMEM((2, 8, 128), f32),
            pltpu.VMEM((16, 128), f32),
            pltpu.VMEM((4, 8, 128), f32),
            pltpu.VMEM((ITERS, 16, 128), f32),
            pltpu.VMEM((ITERS, PLANE, 16, 128), f32),
            pltpu.VMEM((ITERS, 2, 16, 128), f32),
            pltpu.VMEM((ITERS, 2 * NEAR, 16, 128), f32),
            pltpu.VMEM((ITERS, 16, 128), f32),
            pltpu.VMEM((ITERS, 2 * FAR, 16, 128), f32),
            pltpu.VMEM((1, 128), f32),
            pltpu.VMEM((PLANE, 1, 128), f32),
            dma((4,)),
            dma((2 * HALF * UNITS,)),
            dma((3,)),
            dma((4 * UNITS,)),
            dma((16 * UNITS,)),
            dma((1,)),
            dma((3,)),
            dma((ITERS,)),
            dma((ITERS,)),
            dma((ITERS,)),
            dma((ITERS,)),
            dma((ITERS,)),
            dma((ITERS,)),
            dma((1,)),
            dma((1,)),
        ],
        compiler_params=pltpu.CompilerParams(
            collective_id=0, has_side_effects=True, vmem_limit_bytes=60 * 1024 * 1024
        ),
        cost_estimate=pl.CostEstimate(
            flops=2 * wide * (rows_src * cols_all + rows_tgt * cols_tgt),
            bytes_accessed=2 * width * (a + b),
            transcendentals=rows_src * (cols_src + 3 * cols_tgt) + rows_tgt * cols_tgt,
        ),
    )(earlier_vectors, later_vectors)
    vmem = pl.BlockSpec(memory_space=pltpu.VMEM)
    left, right, earlier, later, div = pl.pallas_call(
        hand_out,
        out_shape=tuple(jax.ShapeDtypeStruct(s, f32) for s in ((1, a), (1, b), (1, a), (1, b), (1, 1))),
        in_specs=[vmem],
        out_specs=(vmem,) * 5,
    )(block)
    return left.reshape(a), right.reshape(b), earlier.reshape(a), later.reshape(b), div.reshape(())


def solution(mesh):
    return jax.shard_map(
        per_device,
        mesh=mesh,
        in_specs=(P(("row", "col"), None), P(("row", "col"), None)),
        out_specs=(P(("row", "col")), P(("row", "col")), P(("row", "col")), P(("row", "col")), P()),
        check_vma=False,
    )
```
